512 devices in a mesh: dp: 64 (over x, y, core), segment: 8 (over z).
Axes of the slice: x: 4, y: 8, z: 8, core: 2. Of those that a mesh axis runs over, the one named last changes fastest.
Arguments:
- saved_context: bfloat16 [2048, 128, 640], P(('dp', 'segment')), may hold values from -0.078125 to 0.078125
- cotangent: bfloat16 [2048, 128, 1280], P(('dp', 'segment')), may hold values from -24 to 24
- out_proj: bfloat16 [8, 1280, 640], P('segment'), may hold values from -0.25 to 0.25
- frame_counts: int32 [2048], P(('dp', 'segment')), may hold values from 33 to 128, as said below
- host_segment: int32 [2048], P('dp'), may hold values from 0 to 7, as said below
Outputs:
- frame_grad: bfloat16 [2048, 128, 640], P(('dp', 'segment'))
- weight_grad: bfloat16 [8, 1280, 640], P('segment', 'dp')
The draws below stay inside these ranges and needn't reach their ends.
Inputs may be any that keep to these rules, and one draw needn't show every extreme that they name: `host_segment`: among the 32 utterances of one index of dp, no segment is named more than 6 times and some segment exactly 6 times; the 4 utterances of one device name different segments. `frame_counts`: every device holds an utterance of exactly 128 live frames.
All inputs are finite; a program needn't handle non-finite values.
Results may differ from the reference program's by a relative error of at most 0.001.
Values may be sent and summed in bfloat16 or wider, within the bound.
A program may use at most 64 MiB of HBM per device.

```python
import jax
import jax.numpy as jnp
from jax import lax

C = 1280
HW = 640
FRAMES = 128
UTT_DEV = 4
SLOTS = 6
LAYERS = 8
UTTS = 2048
N_DP = 64
N_SEGMENT = 8


def draw_frame_counts(key, part):
    key = jax.random.fold_in(key, 11)
    first_key, second_key = jax.random.split(key)
    owner_total = UTTS // UTT_DEV
    lengths = jax.random.randint(first_key, (owner_total, UTT_DEV), FRAMES // 4 + 1, FRAMES + 1)
    full_slot = jax.random.randint(second_key, (owner_total, 1), 0, UTT_DEV)
    lengths = jnp.where(jnp.arange(UTT_DEV)[None, :] == full_slot, FRAMES, lengths)
    return lengths.reshape(UTTS).astype(jnp.int32)


def draw_host_segment(key, part):
    key = jax.random.fold_in(key, 23)
    segments = N_SEGMENT
    replicas = N_DP
    extra = SLOTS - UTT_DEV
    subkeys = jax.random.split(key, 3)
    host_order = jax.vmap(lambda sub: jax.random.permutation(sub, segments))(jax.random.split(subkeys[0], replicas))
    owner_order = jax.vmap(lambda sub: jax.random.permutation(sub, segments))(jax.random.split(subkeys[1], replicas))
    hot_count = jax.random.randint(subkeys[2], (replicas, 1), 1, max(1, segments // 4) + 1)
    position = jnp.arange(segments, dtype=jnp.int32)[None, :]
    lowered = ((position >= hot_count) & (position < hot_count + hot_count * extra)).astype(jnp.int32)
    run_loads = UTT_DEV + extra * (position < hot_count).astype(jnp.int32) - lowered
    run_ends = jnp.cumsum(run_loads, axis=1)
    seq_pos = jnp.arange(segments * UTT_DEV, dtype=jnp.int32)
    run_index = jnp.sum((run_ends[:, None, :] <= seq_pos[None, :, None]).astype(jnp.int32), axis=2)
    seq_hosts = jnp.take_along_axis(host_order, run_index, axis=1)
    owner_place = jnp.argsort(owner_order, axis=1).astype(jnp.int32)
    seq_index = jnp.arange(UTT_DEV, dtype=jnp.int32)[None, None, :] * segments + owner_place[:, :, None]
    plan = jnp.take_along_axis(seq_hosts, seq_index.reshape(replicas, segments * UTT_DEV), axis=1)
    return plan.reshape(UTTS).astype(jnp.int32)


def with_spikes(result, rng, source, target, blocks, factor):
    owner, partner = [(jnp.arange(result.shape[dim]) // (result.shape[dim] // blocks)).reshape([-1 if axis == dim else 1 for axis in range(result.ndim)]) for dim in (source, target)]
    chosen = jax.random.permutation(rng, blocks)[partner]
    strong = (owner == chosen) | (owner == (partner + blocks // 2) % blocks)
    return jnp.where(strong, factor * result, result)


def shard_levels(own_key, extent, pieces, least, largest):
    level = 1.0
    for dim, parts in pieces:
        draws = jax.random.uniform(jax.random.fold_in(jax.random.fold_in(own_key, 6), dim), (parts,), jnp.float32, least / len(pieces), largest / len(pieces))
        level = level * jnp.repeat(jnp.exp(draws), extent[dim] // parts).reshape((-1,) + (1,) * (len(extent) - 1 - dim))
    return level


def noise(key, extent, deviation, bound, cuts=(), kind=jnp.bfloat16):
    drawn = jax.random.normal(key, extent, jnp.float32) * deviation
    if len(cuts) > 0:
        drawn = shard_levels(key, extent, cuts, -0.22, 0.18) * drawn
    return jnp.clip(drawn, min=-bound, max=bound).astype(kind)


def gaussian_with(key, dims, scale, bound, cuts, heavy, held_as=jnp.bfloat16):
    values = scale * jax.random.normal(key, dims, jnp.float32)
    if cuts:
        values = values * shard_levels(key, dims, cuts, -0.22, 0.18)
    return jnp.clip(with_spikes(values, jax.random.fold_in(key, 3), *heavy), -bound, bound).astype(held_as)


def setup_inputs(seed: int = 0) -> dict:
    arg_keys = jax.random.split(jax.random.key(seed), 6)
    saved_context = noise(arg_keys[0], (UTTS, FRAMES, HW), ((UTT_DEV * FRAMES * N_DP) ** -0.5), 0.078125, ((0, 512),))
    cotangent = gaussian_with(arg_keys[1], (UTTS, FRAMES, C), 1.0, 24.0, ((0, 512),), (0, 2, 256, 6.0))
    out_proj = noise(arg_keys[2], (LAYERS, C, HW), HW ** -0.5, 0.25, ((0, 8),))
    frame_counts = draw_frame_counts(jax.random.fold_in(arg_keys[5], 71), 0)
    host_segment = draw_host_segment(jax.random.fold_in(arg_keys[5], 71), 0)
    return dict(saved_context=saved_context, cotangent=cotangent, out_proj=out_proj, frame_counts=frame_counts, host_segment=host_segment)


def reference(saved_context, cotangent, out_proj, frame_counts, host_segment):
    live_rows = jnp.arange(FRAMES, dtype=jnp.int32)[None, :] < frame_counts[:, None]
    masked = jnp.where(live_rows[:, :, None], cotangent, jnp.zeros_like(cotangent))

    def per_utterance(totals, scan_item):
        context_one, grad_one, layer_id = scan_item
        weight = lax.dynamic_index_in_dim(out_proj, layer_id, 0, keepdims=False)
        frame_row = jnp.dot(grad_one, weight, preferred_element_type=jnp.float32).astype(jnp.bfloat16)
        layer_term = jnp.dot(grad_one.T, context_one, preferred_element_type=jnp.float32)
        current = lax.dynamic_index_in_dim(totals, layer_id, 0, keepdims=False)
        totals = lax.dynamic_update_index_in_dim(totals, current + layer_term, layer_id, 0)
        return totals, frame_row

    start_totals = jnp.zeros((LAYERS, C, HW), jnp.float32)
    totals, frame_grad = lax.scan(per_utterance, start_totals, (saved_context, masked, host_segment.astype(jnp.int32)))
    return frame_grad, totals.astype(jnp.bfloat16)
```

```python
import functools
import heapq

import jax
import jax.numpy as jnp
from jax import lax
from jax.experimental import pallas as pl
from jax.experimental.pallas import tpu as pltpu
from jax.sharding import PartitionSpec as P

MESH = pl.DeviceIdType.MESH
NX, NY, NC, NZ = 4, 8, 2, 8
C, HW, FR, UD = 1280, 640, 128, 4
KS = 3 * FR
CUT = 256
PIECE = C * 2 // (NX * NY)
WA = 32
ROWS = C // (NX * NY)
WIN = 24


def kernel(host, counts, ctx, cot, w, fg_ref, wg_ref, uctx, ucot, zctx, zcot, kctx, kcot, pctx, pcot, wbuf, t, ray, rax, rbx, rby, r,
           fr, fall, fs, rbl, rbr, rrl, rrr, lsem, zs, zr, cs, cr, ws, wr, gs, gr, fs_s, fs_r):
    dp = lax.axis_index("dp")
    z = lax.axis_index("segment")
    x, y, c = dp // (NY * NC), lax.rem(dp // NC, NY), lax.rem(dp, NC)
    zp, zh = lax.rem(z, 2), z // 2

    def dev(xx=None, yy=None, cc=None, zz=None):
        xx, yy, cc, zz = (b if a is None else a for a, b in ((xx, x), (yy, y), (cc, c), (zz, z)))
        return ((xx * NY + yy) * NC + cc, zz)

    def mod(v, n):
        return lax.rem(v + 2 * n, n)

    z_up, z_dn = dev(zz=mod(z + 1, NZ)), dev(zz=mod(z - 1, NZ))
    x_up, x_dn = dev(xx=mod(x + 1, NX)), dev(xx=mod(x - 1, NX))
    y_up, y_dn = dev(yy=mod(y + 1, NY)), dev(yy=mod(y - 1, NY))
    sib = dev(cc=1 - c)

    bar = pltpu.get_barrier_semaphore()
    partners = [z_up, z_dn, x_up, x_dn, y_up, y_dn, sib]
    for d in (2, 4, 6):
        for cc in (c, 1 - c):
            partners.append(dev(cc=cc, zz=mod(z + d, NZ)))
    for p in partners:
        pl.semaphore_signal(bar, inc=1, device_id=p, device_id_type=MESH)

    load_ctx = pltpu.make_async_copy(ctx, uctx, lsem.at[0])
    load_cot = pltpu.make_async_copy(cot, ucot, lsem.at[1])
    load_ctx.start()
    load_cot.start()
    load_ctx.wait()
    frame = lax.broadcasted_iota(jnp.int32, (FR, HW), 0)
    for u in range(UD):
        uctx[u] = jnp.where(frame < counts[u], uctx[u], jnp.zeros((FR, HW), jnp.bfloat16))

    pl.semaphore_wait(bar, len(partners))

    def rc(src, dst, ssem, rsem, to):
        return pltpu.make_async_remote_copy(src_ref=src, dst_ref=dst, send_sem=ssem, recv_sem=rsem, device_id=to, device_id_type=MESH)

    zc = []
    for k, (lo, at, to) in enumerate(((0, 0, z_up), (2, 2, z_dn))):
        zc.append(rc(cot.at[pl.ds(lo, 2)], zcot.at[pl.ds(at, 2)], zs.at[2 * k], zr.at[2 * k], to))
        zc.append(rc(uctx.at[pl.ds(lo, 2)], zctx.at[pl.ds(at, 2)], zs.at[2 * k + 1], zr.at[2 * k + 1], to))
    for cp in zc:
        cp.start()

    kkp, row0 = x // 2, lax.rem(x, 2) * (C // 2) + y * PIECE
    wsrc = w.at[pl.ds(pl.multiple_of(row0, 16), PIECE)]
    wdst = wbuf.at[x, y]
    is_src = zh == 2 * c + kkp
    wcp = [rc(wsrc, wdst, ws.at[i], wr.at[0], dev(zz=mod(z + d, NZ))) for i, d in enumerate((2, 4, 6))]
    wlocal = pltpu.make_async_copy(wsrc, wdst, lsem.at[2])

    @pl.when(is_src)
    def _():
        wlocal.start()
        for cp in wcp:
            cp.start()
        wlocal.wait()

    @pl.when(jnp.logical_not(is_src))
    def _():
        wcp[0].wait_recv()

    def host_of(zz, u):
        return host[zz * UD + u]

    zl, zrr = mod(z - 1, NZ), mod(z + 1, NZ)

    def find(layer, slot):
        if slot == 0:
            cand = [(host_of(z, u), u) for u in range(4)]
        elif slot == 1:
            cand = [(host_of(zl, u), u) for u in (0, 1)]
        else:
            cand = [(host_of(zrr, u), u) for u in (2, 3)]
        idx, valid = jnp.int32(cand[0][1]), jnp.int32(0)
        for h, at in cand:
            idx = jnp.where(h == layer, jnp.int32(at), idx)
            valid = jnp.where(h == layer, jnp.int32(1), valid)
        return idx, valid

    def fill(dst_cot, dst_ctx, core, slot):
        from_cot, from_ctx = (ucot, uctx) if slot == 0 else (zcot, zctx)
        for kk in range(2):
            idx, valid = find(zp + 4 * core + 2 * kk, slot)
            rows = pl.ds(slot * FR, FR)
            dst_cot[kk, rows, :] = from_cot[idx]
            keep = jnp.full((FR, HW), valid, jnp.int32) > 0
            dst_ctx[kk, rows, :] = jnp.where(keep, from_ctx[idx], jnp.zeros((FR, HW), jnp.bfloat16))

    def core_copies(slot):
        out = []
        for kk in range(2):
            i = 2 * slot + kk
            rows = pl.ds(slot * FR, FR)
            there = pl.ds(KS + slot * FR, FR)
            out.append(rc(pcot.at[kk, rows], kcot.at[kk, there], cs.at[2 * i], cr.at[2 * i], sib))
            out.append(rc(pctx.at[kk, rows], kctx.at[kk, there], cs.at[2 * i + 1], cr.at[2 * i + 1], sib))
        return out

    queue = []
    order = [0]

    def put(gen, when):
        heapq.heappush(queue, (when, order[0], gen))
        order[0] += 1

    def run(until):
        while queue and queue[0][0] < until:
            _, _, gen = heapq.heappop(queue)
            try:
                put(gen, next(gen))
            except StopIteration:
                pass

    pending = []
    wn = [3]

    def wcopy(ref, to):
        i = wn[0]
        wn[0] += 1
        cp = rc(ref, ref, ws.at[i], wr.at[i], to)
        pending.append(cp)
        return cp

    def gather(n, at, me, up, dn, view, halves, t0, step):
        far = n // 2
        ups, dns = [], []
        for s in range(far):
            last = s == far - 1
            for lst, to, sign, hf in ((ups, up, 1, halves[0]), (dns, dn, -1, halves[1])):
                b = mod(me - sign * s, n)
                ref = view(b)
                if last and far > 1:
                    ref = hf(b)
                cp = wcopy(ref, to)
                lst.append(cp)
                if s > 0:
                    lst[s - 1].wait_recv()
                cp.start()
            t0 += step
            yield t0
        ups[-1].wait_recv()
        dns[-1].wait_recv()

    a_rows, b_rows = pl.ds(0, WA), pl.ds(WA, PIECE - WA)

    def weights_a():
        yield from gather(NX, None, x, x_up, x_dn, lambda b: wbuf.at[b, y, a_rows],
                          (lambda b: wbuf.at[b, y, pl.ds(0, 16)], lambda b: wbuf.at[b, y, pl.ds(16, 16)]), 2, 2)
        yield from gather(NY, None, y, y_up, y_dn, lambda b: wbuf.at[:, b, a_rows],
                          (lambda b: wbuf.at[pl.ds(0, 2), b, a_rows], lambda b: wbuf.at[pl.ds(2, 2), b, a_rows]), 6, 4)

    def weights_b():
        yield from gather(NY, None, y, y_up, y_dn, lambda b: wbuf.at[x, b, b_rows],
                          (lambda b: wbuf.at[x, b, pl.ds(WA, 32)], lambda b: wbuf.at[x, b, pl.ds(WA + 32, 16)]), 2, 2)
        yield from gather(NX, None, x, x_up, x_dn, lambda b: wbuf.at[b, :, b_rows],
                          (lambda b: wbuf.at[b, pl.ds(0, 4), b_rows], lambda b: wbuf.at[b, pl.ds(4, 4), b_rows]), 10, 5)

    put(weights_a(), 0)
    put(weights_b(), 0.5)
    run(1)

    load_cot.wait()
    own_core = []
    fill(pcot, pctx, 1 - c, 0)
    own_core += core_copies(0)
    for cp in own_core:
        cp.start()
    fill(kcot, kctx, c, 0)
    run(18)
    for cp in zc:
        cp.wait_recv()
    for slot in (1, 2):
        fill(pcot, pctx, 1 - c, slot)
        cps = core_copies(slot)
        for cp in cps:
            cp.start()
        own_core += cps
    for slot in (1, 2):
        fill(kcot, kctx, c, slot)
    for cp in own_core:
        cp.wait_recv()

    for kk in range(2):
        @pl.loop(0, C // 256)
        def _(i):
            cols = pl.ds(pl.multiple_of(i * 256, 256), 256)
            t[kk, cols, :] = lax.dot_general(kcot[kk, :, cols], kctx[kk], (((0,), (0,)), ((), ())), preferred_element_type=jnp.float32)

    gn = [0]

    def gcopy(src, dst, to):
        i = gn[0]
        gn[0] += 1
        cp = rc(src, dst, gs.at[i], gr.at[i], to)
        pending.append(cp)
        return cp

    def rows_of(xb, yb, n=1):
        return pl.ds(pl.multiple_of((xb * NY + yb) * ROWS, 8), ROWS * n)

    left, right = pl.ds(0, CUT), pl.ds(CUT, HW - CUT)

    def ring(n, me, sign, to, own, slot, t0, step):
        cp = gcopy(own(mod(me - sign, n)), slot(0), to)
        cp.start()
        for s in range(1, n):
            t0 += step
            yield t0
            cp.wait_recv()
            b = mod(me - sign * (s + 1), n)
            here = slot(s - 1)
            here[...] = here[...] + own(b)[...]
            if s < n - 1:
                cp = gcopy(here, slot(s), to)
                cp.start()

    left_a, left_b = [4, 4], [4, 4]

    def part_a(kk, q, t0):
        sign = 1 - 2 * kk
        yield from ring(NY, y, sign, (y_up, y_dn)[kk], lambda b: t.at[kk, rows_of(q, b), left],
                        lambda s: ray.at[kk, s, q], t0, 3.5)
        left_a[kk] -= 1
        if left_a[kk] == 0:
            put(part_a2(kk, t0 + 24.5), t0 + 24.5)

    def part_a2(kk, t0):
        sign = 1 - 2 * kk
        yield from ring(NX, x, sign, (x_up, x_dn)[kk], lambda b: ray.at[kk, NY - 2, b],
                        lambda s: rax.at[kk, s], t0, 3)
        r[kk, :, 0:CUT] = rax[kk, NX - 2]

    def part_b(kk, q, t0):
        sign = 1 - 2 * kk
        yield from ring(NX, x, sign, (x_up, x_dn)[kk], lambda b: t.at[kk, rows_of(b, 2 * q, 2), right],
                        lambda s: rbx.at[kk, s, pl.ds(2 * q * ROWS, 2 * ROWS)], t0, 9.8)
        left_b[kk] -= 1
        if left_b[kk] == 0:
            put(part_b2(kk, t0 + 29.4), t0 + 29.4)

    def part_b2(kk, t0):
        sign = 1 - 2 * kk
        yield from ring(NY, y, sign, (y_up, y_dn)[kk],
                        lambda b: rbx.at[kk, NX - 2, pl.ds(pl.multiple_of(b * ROWS, 8), ROWS)],
                        lambda s: rby.at[kk, s], t0, 2.5)
        r[kk, :, CUT:HW] = rby[kk, NY - 2]

    base = 30.0
    for kk in range(2):
        for q in range(4):
            put(part_b(kk, q, base + 0.1 * q), base)
            put(part_a(kk, q, base + 0.1 * q), base)
    run(base + 1)

    def outputs():
        for kk in range(2):
            @pl.loop(0, 3)
            def _(i):
                rows = pl.ds(pl.multiple_of(i * FR, FR), FR)
                fall[2 * c + kk, rows, :] = jnp.dot(kcot[kk, rows, :], wbuf[pl.ds(2 * kk, 2)].reshape(C, HW),
                                                    preferred_element_type=jnp.float32).astype(jnp.bfloat16)
                more = pl.ds(pl.multiple_of(KS + i * FR, FR), FR)
                fs[kk, rows, :] = jnp.dot(kcot[kk, more, :], wbuf[pl.ds(2 * kk, 2)].reshape(C, HW),
                                          preferred_element_type=jnp.float32).astype(jnp.bfloat16)
        back = rc(fs, fall.at[pl.ds(2 * c, 2)], fs_s.at[0], fs_r.at[0], sib)
        back.start()
        pending.append(back)
        yield base + 12
        back.wait_recv()
        for u in (0, 1):
            rbl[u] = fall[host_of(zl, u) >> 1, FR:2 * FR, :]
            rbr[u] = fall[host_of(zrr, u + 2) >> 1, 2 * FR:3 * FR, :]
        to_dn = rc(rbl, rrr, fs_s.at[1], fs_r.at[1], z_dn)
        to_up = rc(rbr, rrl, fs_s.at[2], fs_r.at[2], z_up)
        to_dn.start()
        to_up.start()
        pending.extend((to_dn, to_up))
        yield base + 24
        to_dn.wait_recv()
        to_up.wait_recv()
        for u in range(UD):
            h = host_of(z, u)
            mine = jnp.full((FR, HW), h & 1, jnp.int32) == zp
            got = rrr[u] if u < 2 else rrl[u - 2]
            val = jnp.where(mine, fall[h >> 1, 0:FR, :], got)
            fg_ref[u] = jnp.where(frame < counts[u], val, jnp.zeros((FR, HW), jnp.bfloat16))

    run(18 + 12)
    put(outputs(), base + 2)
    run(base + 1000)

    last = []
    for kk in range(2):
        layer = zp + 4 * c + 2 * kk
        for cc in range(2):
            here = r.at[kk, pl.ds(16 * cc, WIN)]
            send = rc(here, fr.at[zh], fs_s.at[3 + 2 * kk + cc], fs_r.at[3 + zh], dev(cc=cc, zz=layer))
            same = jnp.logical_and(layer == z, c == cc)
            last.append((send, same))

            @pl.when(jnp.logical_not(same))
            def _():
                send.start()

            @pl.when(same)
            def _():
                fr[zh] = here[...]
    for i in range(4):
        got = rc(r.at[0, pl.ds(0, WIN)], fr.at[i], fs_s.at[3], fs_r.at[3 + i], sib)

        @pl.when(jnp.logical_not(jnp.logical_and(zh == i, z // 4 == c)))
        def _():
            got.wait_recv()
    first = fr[0, 0:20, :] + fr[1, 0:20, :] + fr[2, 0:20, :] + fr[3, 0:20, :]
    second = fr[0, 4:24, :] + fr[1, 4:24, :] + fr[2, 4:24, :] + fr[3, 4:24, :]
    wg_ref[...] = jnp.where(jnp.full((20, HW), c, jnp.int32) == 0, first, second).astype(jnp.bfloat16)

    for send, same in last:
        @pl.when(jnp.logical_not(same))
        def _():
            send.wait_send()

    for cp in zc + own_core + pending:
        cp.wait_send()

    @pl.when(is_src)
    def _():
        for cp in wcp:
            cp.wait_send()


def local(saved_context, cotangent, out_proj, frame_counts, host_segment):
    bf, f32, dma = jnp.bfloat16, jnp.float32, pltpu.SemaphoreType.DMA
    smem, vmem, hbm = (pl.BlockSpec(memory_space=m) for m in (pltpu.SMEM, pltpu.VMEM, pl.ANY))
    fg, wg = pl.pallas_call(
        kernel,
        name="backward",
        out_shape=(jax.ShapeDtypeStruct((UD, FR, HW), bf), jax.ShapeDtypeStruct((20, HW), bf)),
        in_specs=[smem, smem, hbm, hbm, hbm],
        out_specs=(vmem, vmem),
        scratch_shapes=[
            pltpu.VMEM((UD, FR, HW), bf),
            pltpu.VMEM((UD, FR, C), bf),
            pltpu.VMEM((4, FR, HW), bf),
            pltpu.VMEM((4, FR, C), bf),
            pltpu.VMEM((2, 2 * KS, HW), bf),
            pltpu.VMEM((2, 2 * KS, C), bf),
            pltpu.VMEM((2, KS, HW), bf),
            pltpu.VMEM((2, KS, C), bf),
            pltpu.VMEM((NX, NY, PIECE, HW), bf),
            pltpu.VMEM((2, C, HW), f32),
            pltpu.VMEM((2, NY - 1, NX, ROWS, CUT), f32),
            pltpu.VMEM((2, NX - 1, ROWS, CUT), f32),
            pltpu.VMEM((2, NX - 1, NY * ROWS, HW - CUT), f32),
            pltpu.VMEM((2, NY - 1, ROWS, HW - CUT), f32),
            pltpu.VMEM((2, ROWS, HW), f32),
            pltpu.VMEM((4, WIN, HW), f32),
            pltpu.VMEM((4, KS, HW), bf),
            pltpu.VMEM((2, KS, HW), bf),
            pltpu.VMEM((2, FR, HW), bf),
            pltpu.VMEM((2, FR, HW), bf),
            pltpu.VMEM((2, FR, HW), bf),
            pltpu.VMEM((2, FR, HW), bf),
            dma((3,)),
            dma((4,)), dma((4,)),
            dma((12,)), dma((12,)),
            dma((32,)), dma((32,)),
            dma((120,)), dma((120,)),
            dma((8,)), dma((8,)),
        ],
        compiler_params=pltpu.CompilerParams(collective_id=0, has_side_effects=True, vmem_limit_bytes=56 << 20),
    )(host_segment, frame_counts, saved_context, cotangent, out_proj[0])
    return fg, wg[None]


def solution(mesh):
    placed = (
        P(("dp", "segment"), None, None),
        P(("dp", "segment"), None, None),
        P("segment", None, None),
        P(("dp", "segment")),
        P("dp"),
    )
    return jax.shard_map(
        local,
        mesh=mesh,
        in_specs=placed,
        out_specs=(P(("dp", "segment"), None, None), P("segment", "dp", None)),
        check_vma=False,
    )
```

```python
import functools
import heapq

import jax
import jax.numpy as jnp
from jax import lax
from jax.experimental import pallas as pl
from jax.experimental.pallas import tpu as pltpu
from jax.sharding import PartitionSpec as P

MESH = pl.DeviceIdType.MESH
NX, NY, NC, NZ = 4, 8, 2, 8
C, HW, FR, UD = 1280, 640, 128, 4
KS = 3 * FR
CUT = 256
PIECE = C * 2 // (NX * NY)
WA = 32
ROWS = C // (NX * NY)
WIN = 24


def kernel(host, counts, ctx, cot, w, fg_ref, wg_ref, uctx, ucot, zctx, zcot, kctx, kcot, pctx, pcot, wbuf, t, ray, rax, rbx, rby, r,
           fr, fall, fs, rbl, rbr, rrl, rrr, lsem, zs, zr, cs, cr, ws, wr, gs, gr, fs_s, fs_r):
    dp = lax.axis_index("dp")
    z = lax.axis_index("segment")
    x, y, c = dp // (NY * NC), lax.rem(dp // NC, NY), lax.rem(dp, NC)
    zp, zh = lax.rem(z, 2), z // 2

    def dev(xx=None, yy=None, cc=None, zz=None):
        xx, yy, cc, zz = (b if a is None else a for a, b in ((xx, x), (yy, y), (cc, c), (zz, z)))
        return ((xx * NY + yy) * NC + cc, zz)

    def mod(v, n):
        return lax.rem(v + 2 * n, n)

    z_up, z_dn = dev(zz=mod(z + 1, NZ)), dev(zz=mod(z - 1, NZ))
    x_up, x_dn = dev(xx=mod(x + 1, NX)), dev(xx=mod(x - 1, NX))
    y_up, y_dn = dev(yy=mod(y + 1, NY)), dev(yy=mod(y - 1, NY))
    sib = dev(cc=1 - c)

    bar = pltpu.get_barrier_semaphore()
    partners = [z_up, z_dn, x_up, x_dn, y_up, y_dn, sib]
    for d in (2, 4, 6):
        for cc in (c, 1 - c):
            partners.append(dev(cc=cc, zz=mod(z + d, NZ)))
    for p in partners:
        pl.semaphore_signal(bar, inc=1, device_id=p, device_id_type=MESH)

    load_ctx = pltpu.make_async_copy(ctx, uctx, lsem.at[0])
    load_cot = pltpu.make_async_copy(cot, ucot, lsem.at[1])
    load_ctx.start()
    load_cot.start()
    pl.semaphore_wait(bar, len(partners))

    def rc(src, dst, ssem, rsem, to):
        return pltpu.make_async_remote_copy(src_ref=src, dst_ref=dst, send_sem=ssem, recv_sem=rsem, device_id=to, device_id_type=MESH)

    kkp, row0 = x // 2, lax.rem(x, 2) * (C // 2) + y * PIECE
    wsrc = w.at[pl.ds(pl.multiple_of(row0, 16), PIECE)]
    wdst = wbuf.at[x, y]
    is_src = zh == 2 * c + kkp
    wcp = [rc(wsrc, wdst, ws.at[i], wr.at[0], dev(zz=mod(z + d, NZ))) for i, d in enumerate((2, 4, 6))]
    wlocal = pltpu.make_async_copy(wsrc, wdst, lsem.at[2])

    @pl.when(is_src)
    def _():
        for cp in wcp:
            cp.start()
        wlocal.start()

    zcot_cp, zctx_cp = [], []
    for k, (lo, at, to) in enumerate(((0, 0, z_up), (2, 2, z_dn))):
        zcot_cp.append(rc(cot.at[pl.ds(lo, 2)], zcot.at[pl.ds(at, 2)], zs.at[2 * k], zr.at[2 * k], to))
        zctx_cp.append(rc(uctx.at[pl.ds(lo, 2)], zctx.at[pl.ds(at, 2)], zs.at[2 * k + 1], zr.at[2 * k + 1], to))
    for cp in zcot_cp:
        cp.start()

    load_ctx.wait()
    frame = lax.broadcasted_iota(jnp.int32, (FR, HW), 0)
    for u in range(UD):
        uctx[u] = jnp.where(frame < counts[u], uctx[u], jnp.zeros((FR, HW), jnp.bfloat16))

    queue = []
    order = [0]

    def put(gen, when):
        heapq.heappush(queue, (when, order[0], gen))
        order[0] += 1

    def run(until):
        while queue and queue[0][0] < until:
            _, _, gen = heapq.heappop(queue)
            try:
                put(gen, next(gen))
            except StopIteration:
                pass

    def host_of(zz, u):
        return host[zz * UD + u]

    zl, zrr = mod(z - 1, NZ), mod(z + 1, NZ)

    def find(layer, slot):
        if slot == 0:
            cand = [(host_of(z, u), u) for u in range(4)]
        elif slot == 1:
            cand = [(host_of(zl, u), u) for u in (0, 1)]
        else:
            cand = [(host_of(zrr, u), u) for u in (2, 3)]
        idx, valid = jnp.int32(cand[0][1]), jnp.int32(0)
        for h, at in cand:
            idx = jnp.where(h == layer, jnp.int32(at), idx)
            valid = jnp.where(h == layer, jnp.int32(1), valid)
        return idx, valid

    def fill_cot(dst, core, slot):
        for kk in range(2):
            idx, _ = find(zp + 4 * core + 2 * kk, slot)
            dst[kk, slot * FR:(slot + 1) * FR, :] = (ucot if slot == 0 else zcot)[idx]

    def fill_ctx(dst, core, slot):
        for kk in range(2):
            idx, valid = find(zp + 4 * core + 2 * kk, slot)
            keep = jnp.full((FR, HW), valid, jnp.int32) > 0
            val = (uctx if slot == 0 else zctx)[idx]
            dst[kk, slot * FR:(slot + 1) * FR, :] = jnp.where(keep, val, jnp.zeros((FR, HW), jnp.bfloat16))

    own_core = []

    def core_send(src, dst, lo, hi):
        for kk in range(2):
            i = len(own_core)
            own_core.append(rc(src.at[kk, pl.ds(lo * FR, (hi - lo) * FR)], dst.at[kk, pl.ds(KS + lo * FR, (hi - lo) * FR)],
                               cs.at[i], cr.at[i], sib))
            own_core[-1].start()

    pending = []
    wn = [3]

    def wcopy(ref, to):
        i = wn[0]
        wn[0] += 1
        cp = rc(ref, ref, ws.at[i], wr.at[i], to)
        pending.append(cp)
        return cp

    HOP = 2.7

    def spread(n, me, up, dn, view, half, done, t0):
        far = n // 2
        ups, dns = [wcopy(view(me), up)], [wcopy(view(me), dn)]
        ups[0].start()
        dns[0].start()
        for s in range(1, far):
            for lst, to, sign in ((ups, up, 1), (dns, dn, -1)):
                t = t0 + HOP * s
                yield t
                ref = view(mod(me - sign * s, n))
                if s == far - 1:
                    ref = half(mod(me - sign * s, n), sign)
                cp = wcopy(ref, to)
                lst[-1].wait_recv()
                cp.start()
                lst.append(cp)
                done(-sign * s, t)
        t = t0 + HOP * far
        yield t
        ups[-1].wait_recv()
        dns[-1].wait_recv()
        done(far, t)

    def nothing(delta, t):
        pass

    a_rows, b_rows = pl.ds(0, WA), pl.ds(WA, PIECE - WA)

    def spread_ay(delta, t):
        b = mod(x + delta, NX)
        put(spread(NY, y, y_up, y_dn, lambda k: wbuf.at[b, k, a_rows],
                   lambda k, sign: wbuf.at[b, k, pl.ds(0 if sign > 0 else 16, 16)], nothing, t), t)

    def spread_bx(delta, t):
        b = mod(y + delta, NY)

        def half(k, sign):
            if (sign > 0) == (delta % 2 == 0):
                return wbuf.at[k, b, pl.ds(WA, 32)]
            return wbuf.at[k, b, pl.ds(WA + 32, 16)]

        put(spread(NX, x, x_up, x_dn, lambda k: wbuf.at[k, b, b_rows], half, nothing, t), t)

    def weights():
        @pl.when(is_src)
        def _():
            wlocal.wait()

        @pl.when(jnp.logical_not(is_src))
        def _():
            wcp[0].wait_recv()

        put(spread(NX, x, x_up, x_dn, lambda b: wbuf.at[b, y, a_rows],
                   lambda b, sign: wbuf.at[b, y, pl.ds(0 if sign > 0 else 16, 16)], spread_ay, W0), W0)
        put(spread(NY, y, y_up, y_dn, lambda b: wbuf.at[x, b, b_rows],
                   lambda b, sign: wbuf.at[x, b, pl.ds(WA, 32) if sign > 0 else pl.ds(WA + 32, 16)], spread_bx, W0), W0)
        spread_ay(0, W0)
        spread_bx(0, W0)
        yield W0

    def send_ctx():
        for cp in zctx_cp:
            cp.start()
        yield 0

    W0 = 5.0
    put(weights(), W0)
    put(send_ctx(), 8.0)

    load_cot.wait()
    fill_cot(pcot, 1 - c, 0)
    core_send(pcot, kcot, 0, 1)
    fill_ctx(pctx, 1 - c, 0)
    core_send(pctx, kctx, 0, 1)
    fill_cot(kcot, c, 0)
    fill_ctx(kctx, c, 0)
    run(14.0)
    for cp in zcot_cp:
        cp.wait_recv()
    for slot in (1, 2):
        fill_cot(pcot, 1 - c, slot)
    core_send(pcot, kcot, 1, 3)
    for slot in (1, 2):
        fill_cot(kcot, c, slot)
    run(20.0)
    for cp in zctx_cp:
        cp.wait_recv()
    for slot in (1, 2):
        fill_ctx(pctx, 1 - c, slot)
    core_send(pctx, kctx, 1, 3)
    for slot in (1, 2):
        fill_ctx(kctx, c, slot)
    run(22.0)
    for cp in own_core:
        cp.wait_recv()

    for kk in range(2):
        @pl.loop(0, C // 256)
        def _(i):
            cols = pl.ds(pl.multiple_of(i * 256, 256), 256)
            t[kk, cols, :] = lax.dot_general(kcot[kk, :, cols], kctx[kk], (((0,), (0,)), ((), ())), preferred_element_type=jnp.float32)

    gn = [0]

    def gcopy(src, dst, to):
        i = gn[0]
        gn[0] += 1
        cp = rc(src, dst, gs.at[i], gr.at[i], to)
        pending.append(cp)
        cp.start()
        return cp

    def rows_of(xb, yb):
        return pl.ds(pl.multiple_of((xb * NY + yb) * ROWS, 8), ROWS)

    left, right = pl.ds(0, CUT), pl.ds(CUT, HW - CUT)

    class Chains:
        def __init__(self, n, me, d, to, slot):
            self.n, self.me, self.d, self.to, self.slot = n, me, d, to, slot
            self.last = {1: None, -1: None}

        @staticmethod
        def deltas(n):
            out = [n // 2]
            for k in range(n // 2 - 1, 0, -1):
                out += [-k, k]
            return out + [0]

        def step(self, k, own):
            half = self.n // 2
            if k == 0:
                for way in (1, -1):
                    self.last[way].wait_recv()
                res = self.slot(1, half - 1)
                res[...] = own[...] + res[...] + self.slot(-1, half - 2)[...]
                return res
            way = 1 if k > 0 else -1
            length = half if way > 0 else half - 1
            s = length - abs(k)
            src = own
            if s > 0:
                self.last[way].wait_recv()
                src = self.slot(way, s - 1)
                src[...] = src[...] + own[...]
            self.last[way] = gcopy(src, self.slot(way, s), self.to[way * self.d])
            return None

    x_to, y_to = {1: x_up, -1: x_dn}, {1: y_up, -1: y_dn}

    def slots(ref, half):
        return lambda way, s: ref.at[s if way > 0 else half + s]

    base = 25.0

    def chain_a(kk, j, second):
        d = 1 - 2 * kk
        k2 = Chains.deltas(NX)[j]
        q = mod(x + d * k2, NX)
        ring = Chains(NY, y, d, y_to, slots(ray.at[kk, j], NY // 2))
        t0 = base + 4.5 * j
        for i, k in enumerate(Chains.deltas(NY)):
            got = ring.step(k, t.at[kk, rows_of(q, mod(y + d * k, NY)), left])
            if k < 0 or k == 1:
                yield t0 + 3.6 * (i // 2 + 1)
        got = second.step(k2, got)
        if k2 == 0:
            r[kk, :, 0:CUT] = got[...]

    def chain_b(kk, j, second):
        d = 1 - 2 * kk
        k2 = Chains.deltas(NY)[j]
        q = mod(y + d * k2, NY)
        ring = Chains(NX, x, d, x_to, slots(rbx.at[kk, j], NX // 2))
        t0 = base + 3.7 * j
        for i, k in enumerate(Chains.deltas(NX)):
            got = ring.step(k, t.at[kk, rows_of(mod(x + d * k, NX), q), right])
            if k == -1:
                yield t0 + 4.5
            elif k == 1:
                yield t0 + 8.5
        got = second.step(k2, got)
        if k2 == 0:
            r[kk, :, CUT:HW] = got[...]

    a_second = [Chains(NX, x, 1 - 2 * kk, x_to, slots(rax.at[kk], NX // 2)) for kk in range(2)]
    b_second = [Chains(NY, y, 1 - 2 * kk, y_to, slots(rby.at[kk], NY // 2)) for kk in range(2)]
    for j in range(8):
        for kk in range(2):
            put(chain_b(kk, j, b_second[kk]), base + max(0, 3.7 * (j - 2)))
    for j in range(4):
        for kk in range(2):
            put(chain_a(kk, j, a_second[kk]), base + max(0, 5.7 * (j - 2)))
    run(base + 0.1)
    run(base + 2.0)

    def outputs():
        for kk in range(2):
            @pl.loop(0, 3)
            def _(i):
                rows = pl.ds(pl.multiple_of(i * FR, FR), FR)
                fall[2 * c + kk, rows, :] = jnp.dot(kcot[kk, rows, :], wbuf[pl.ds(2 * kk, 2)].reshape(C, HW),
                                                    preferred_element_type=jnp.float32).astype(jnp.bfloat16)
                more = pl.ds(pl.multiple_of(KS + i * FR, FR), FR)
                fs[kk, rows, :] = jnp.dot(kcot[kk, more, :], wbuf[pl.ds(2 * kk, 2)].reshape(C, HW),
                                          preferred_element_type=jnp.float32).astype(jnp.bfloat16)
            if kk == 0:
                yield base + 9
        back = rc(fs, fall.at[pl.ds(2 * c, 2)], fs_s.at[0], fs_r.at[0], sib)
        back.start()
        pending.append(back)
        yield base + 14
        back.wait_recv()
        for u in (0, 1):
            rbl[u] = fall[host_of(zl, u) >> 1, FR:2 * FR, :]
            rbr[u] = fall[host_of(zrr, u + 2) >> 1, 2 * FR:3 * FR, :]
        to_dn = rc(rbl, rrr, fs_s.at[1], fs_r.at[1], z_dn)
        to_up = rc(rbr, rrl, fs_s.at[2], fs_r.at[2], z_up)
        to_dn.start()
        to_up.start()
        pending.extend((to_dn, to_up))
        yield base + 26
        to_dn.wait_recv()
        to_up.wait_recv()
        for u in range(UD):
            h = host_of(z, u)
            mine = jnp.full((FR, HW), h & 1, jnp.int32) == zp
            got = rrr[u] if u < 2 else rrl[u - 2]
            val = jnp.where(mine, fall[h >> 1, 0:FR, :], got)
            fg_ref[u] = jnp.where(frame < counts[u], val, jnp.zeros((FR, HW), jnp.bfloat16))

    put(outputs(), base + 5)
    run(base + 1000)

    last = []
    for kk in range(2):
        layer = zp + 4 * c + 2 * kk
        for cc in range(2):
            here = r.at[kk, pl.ds(16 * cc, WIN)]
            send = rc(here, fr.at[zh], fs_s.at[3 + 2 * kk + cc], fs_r.at[3 + zh], dev(cc=cc, zz=layer))
            same = jnp.logical_and(layer == z, c == cc)
            last.append((send, same))

            @pl.when(jnp.logical_not(same))
            def _():
                send.start()

            @pl.when(same)
            def _():
                fr[zh] = here[...]
    for i in range(4):
        got = rc(r.at[0, pl.ds(0, WIN)], fr.at[i], fs_s.at[3], fs_r.at[3 + i], sib)

        @pl.when(jnp.logical_not(jnp.logical_and(zh == i, z // 4 == c)))
        def _():
            got.wait_recv()
    first = fr[0, 0:20, :] + fr[1, 0:20, :] + fr[2, 0:20, :] + fr[3, 0:20, :]
    second = fr[0, 4:24, :] + fr[1, 4:24, :] + fr[2, 4:24, :] + fr[3, 4:24, :]
    wg_ref[...] = jnp.where(jnp.full((20, HW), c, jnp.int32) == 0, first, second).astype(jnp.bfloat16)

    for send, same in last:
        @pl.when(jnp.logical_not(same))
        def _():
            send.wait_send()

    for cp in zcot_cp + zctx_cp + own_core + pending:
        cp.wait_send()

    @pl.when(is_src)
    def _():
        for cp in wcp:
            cp.wait_send()


def local(saved_context, cotangent, out_proj, frame_counts, host_segment):
    bf, f32, dma = jnp.bfloat16, jnp.float32, pltpu.SemaphoreType.DMA
    smem, vmem, hbm = (pl.BlockSpec(memory_space=m) for m in (pltpu.SMEM, pltpu.VMEM, pl.ANY))
    fg, wg = pl.pallas_call(
        kernel,
        name="backward",
        out_shape=(jax.ShapeDtypeStruct((UD, FR, HW), bf), jax.ShapeDtypeStruct((20, HW), bf)),
        in_specs=[smem, smem, hbm, hbm, hbm],
        out_specs=(vmem, vmem),
        scratch_shapes=[
            pltpu.VMEM((UD, FR, HW), bf),
            pltpu.VMEM((UD, FR, C), bf),
            pltpu.VMEM((4, FR, HW), bf),
            pltpu.VMEM((4, FR, C), bf),
            pltpu.VMEM((2, 2 * KS, HW), bf),
            pltpu.VMEM((2, 2 * KS, C), bf),
            pltpu.VMEM((2, KS, HW), bf),
            pltpu.VMEM((2, KS, C), bf),
            pltpu.VMEM((NX, NY, PIECE, HW), bf),
            pltpu.VMEM((2, C, HW), f32),
            pltpu.VMEM((2, NX, NY - 1, ROWS, CUT), f32),
            pltpu.VMEM((2, NX - 1, ROWS, CUT), f32),
            pltpu.VMEM((2, NY, NX - 1, ROWS, HW - CUT), f32),
            pltpu.VMEM((2, NY - 1, ROWS, HW - CUT), f32),
            pltpu.VMEM((2, ROWS, HW), f32),
            pltpu.VMEM((4, WIN, HW), f32),
            pltpu.VMEM((4, KS, HW), bf),
            pltpu.VMEM((2, KS, HW), bf),
            pltpu.VMEM((2, FR, HW), bf),
            pltpu.VMEM((2, FR, HW), bf),
            pltpu.VMEM((2, FR, HW), bf),
            pltpu.VMEM((2, FR, HW), bf),
            dma((3,)),
            dma((4,)), dma((4,)),
            dma((12,)), dma((12,)),
            dma((80,)), dma((80,)),
            dma((128,)), dma((128,)),
            dma((8,)), dma((8,)),
        ],
        compiler_params=pltpu.CompilerParams(collective_id=0, has_side_effects=True, vmem_limit_bytes=56 << 20),
    )(host_segment, frame_counts, saved_context, cotangent, out_proj[0])
    return fg, wg[None]


def solution(mesh):
    placed = (
        P(("dp", "segment"), None, None),
        P(("dp", "segment"), None, None),
        P("segment", None, None),
        P(("dp", "segment")),
        P("dp"),
    )
    return jax.shard_map(
        local,
        mesh=mesh,
        in_specs=placed,
        out_specs=(P(("dp", "segment"), None, None), P("segment", "dp", None)),
        check_vma=False,
    )
```

```python
import functools
import heapq

import jax
import jax.numpy as jnp
from jax import lax
from jax.experimental import pallas as pl
from jax.experimental.pallas import tpu as pltpu
from jax.sharding import PartitionSpec as P

MESH = pl.DeviceIdType.MESH
NX, NY, NC, NZ = 4, 8, 2, 8
C, HW, FR, UD = 1280, 640, 128, 4
KS = 3 * FR
CUT = 256
PIECE = C * 2 // (NX * NY)
WA = 32
ROWS = C // (NX * NY)
WIN = 24


def kernel(host, counts, ctx, cot, w, fg_ref, wg_ref, uctx, ucot, zctxa, zctxb, zcot, kctxa, kctxb, kcot, pctxa, pctxb, pcot, wbuf, ta, tb, ray, rax, rbx, rby,
           fra, frb, fall, fs, rbl, rbr, rrl, rrr, lsem, zs, zr, cs, cr, ws, wr, gs, gr, fs_s, fs_r, ls, lr):
    kctx, pctx, t, fr = (kctxa, kctxb), (pctxa, pctxb), (ta, tb), (fra, frb)
    dp = lax.axis_index("dp")
    z = lax.axis_index("segment")
    x, y, c = dp // (NY * NC), lax.rem(dp // NC, NY), lax.rem(dp, NC)
    zp, zh = lax.rem(z, 2), z // 2

    def dev(xx=None, yy=None, cc=None, zz=None):
        xx, yy, cc, zz = (b if a is None else a for a, b in ((xx, x), (yy, y), (cc, c), (zz, z)))
        return ((xx * NY + yy) * NC + cc, zz)

    def mod(v, n):
        return lax.rem(v + 2 * n, n)

    z_up, z_dn = dev(zz=mod(z + 1, NZ)), dev(zz=mod(z - 1, NZ))
    x_up, x_dn = dev(xx=mod(x + 1, NX)), dev(xx=mod(x - 1, NX))
    y_up, y_dn = dev(yy=mod(y + 1, NY)), dev(yy=mod(y - 1, NY))
    sib = dev(cc=1 - c)

    bar = pltpu.get_barrier_semaphore()
    x_far, y_up2, y_dn2 = dev(xx=mod(x + 2, NX)), dev(yy=mod(y + 2, NY)), dev(yy=mod(y - 2, NY))
    partners = [z_up, z_dn, x_up, x_dn, y_up, y_dn, sib, x_far, y_up2, y_dn2]
    for d in (2, 4, 6):
        for cc in (c, 1 - c):
            partners.append(dev(cc=cc, zz=mod(z + d, NZ)))
    for p in partners:
        pl.semaphore_signal(bar, inc=1, device_id=p, device_id_type=MESH)

    load_ctx = pltpu.make_async_copy(ctx, uctx, lsem.at[0])
    load_cot = pltpu.make_async_copy(cot, ucot, lsem.at[1])
    load_ctx.start()
    load_cot.start()
    pl.semaphore_wait(bar, len(partners))

    def rc(src, dst, ssem, rsem, to):
        return pltpu.make_async_remote_copy(src_ref=src, dst_ref=dst, send_sem=ssem, recv_sem=rsem, device_id=to, device_id_type=MESH)

    kkp, row0 = x // 2, lax.rem(x, 2) * (C // 2) + y * PIECE
    wsrc = w.at[pl.ds(pl.multiple_of(row0, 16), PIECE)]
    wdst = wbuf.at[x, y]
    is_src = zh == 2 * c + kkp
    wcp = [rc(wsrc, wdst, ws.at[i], wr.at[0], dev(zz=mod(z + d, NZ))) for i, d in enumerate((2, 4, 6))]
    wlocal = pltpu.make_async_copy(wsrc, wdst, lsem.at[2])

    @pl.when(is_src)
    def _():
        for cp in wcp:
            cp.start()
        wlocal.start()

    left, right = pl.ds(0, CUT), pl.ds(CUT, HW - CUT)
    zcot_cp, zctxa_cp, zctxb_cp = [], [], []
    nz = [0]

    def zcopy(src, dst, to):
        i = nz[0]
        nz[0] += 1
        return rc(src, dst, zs.at[i], zr.at[i], to)

    for u in range(UD):
        to = z_up if u < 2 else z_dn
        for rows in (pl.ds(0, FR // 2), pl.ds(FR // 2, FR // 2)):
            zcot_cp.append(zcopy(cot.at[u, rows], zcot.at[u, rows], to))
        zctxa_cp.append(zcopy(uctx.at[u, :, left], zctxa.at[u], to))
        zctxb_cp.append(zcopy(uctx.at[u, :, right], zctxb.at[u], to))
    for cp in zcot_cp:
        cp.start()

    load_ctx.wait()
    frame = lax.broadcasted_iota(jnp.int32, (FR, HW), 0)
    for u in range(UD):
        uctx[u] = jnp.where(frame < counts[u], uctx[u], jnp.zeros((FR, HW), jnp.bfloat16))

    queue = []
    order = [0]

    def put(gen, when):
        heapq.heappush(queue, (when, order[0], gen))
        order[0] += 1

    def run(until):
        while queue and queue[0][0] < until:
            _, _, gen = heapq.heappop(queue)
            try:
                put(gen, next(gen))
            except StopIteration:
                pass

    def host_of(zz, u):
        return host[zz * UD + u]

    zl, zrr = mod(z - 1, NZ), mod(z + 1, NZ)

    def find(layer, slot):
        if slot == 0:
            cand = [(host_of(z, u), u) for u in range(4)]
        elif slot == 1:
            cand = [(host_of(zl, u), u) for u in (0, 1)]
        else:
            cand = [(host_of(zrr, u), u) for u in (2, 3)]
        idx, valid = jnp.int32(cand[0][1]), jnp.int32(0)
        for h, at in cand:
            idx = jnp.where(h == layer, jnp.int32(at), idx)
            valid = jnp.where(h == layer, jnp.int32(1), valid)
        return idx, valid

    def fill_cot(dst, core, slot):
        for kk in range(2):
            idx, _ = find(zp + 4 * core + 2 * kk, slot)
            dst[kk, slot * FR:(slot + 1) * FR, :] = (ucot if slot == 0 else zcot)[idx]

    def fill_ctx(dst, core, slot, part):
        cols = slice(0, CUT) if part == 0 else slice(CUT, HW)
        for kk in range(2):
            idx, valid = find(zp + 4 * core + 2 * kk, slot)
            val = uctx[idx, :, cols] if slot == 0 else (zctxa, zctxb)[part][idx]
            keep = jnp.full(val.shape, valid, jnp.int32) > 0
            dst[part][kk, slot * FR:(slot + 1) * FR, :] = jnp.where(keep, val, jnp.zeros_like(val))

    own_core = []

    def core_send(src, dst, lo, hi):
        for kk in range(2):
            i = len(own_core)
            own_core.append(rc(src.at[kk, pl.ds(lo * FR, (hi - lo) * FR)], dst.at[kk, pl.ds(KS + lo * FR, (hi - lo) * FR)],
                               cs.at[i], cr.at[i], sib))
            own_core[-1].start()

    pending = []
    wn = [3]

    spreading = [0]

    def track(gen):
        spreading[0] += 1
        yield from gen
        spreading[0] -= 1

    def wcopy(ref, to):
        i = wn[0]
        wn[0] += 1
        cp = rc(ref, ref, ws.at[i], wr.at[i], to)
        pending.append(cp)
        return cp

    HOP = 4.5

    def spread(n, me, up, dn, view, half, done, t0):
        far = n // 2
        ups, dns = [wcopy(view(me), up)], [wcopy(view(me), dn)]
        ups[0].start()
        dns[0].start()
        for s in range(1, far):
            for lst, to, sign in ((ups, up, 1), (dns, dn, -1)):
                t = t0 + HOP * s
                yield t
                ref = view(mod(me - sign * s, n))
                if s == far - 1:
                    ref = half(mod(me - sign * s, n), sign)
                cp = wcopy(ref, to)
                lst[-1].wait_recv()
                cp.start()
                lst.append(cp)
                done(-sign * s, t)
        t = t0 + HOP * far
        yield t
        ups[-1].wait_recv()
        dns[-1].wait_recv()
        done(far, t)

    def nothing(delta, t):
        pass

    def spread_x(view, done, t0):
        cps = [wcopy(view(x), to) for to in (x_up, x_dn, x_far)]
        for cp in cps:
            cp.start()
        for cp, delta in zip(cps, (-1, 1, 2)):
            yield t0 + HOP
            cp.wait_recv()
            done(delta, t0 + HOP)

    def spread_y(view, half, done, t0):
        cps = {k: wcopy(view(y), to) for k, to in ((1, y_up), (-1, y_dn), (2, y_up2), (-2, y_dn2))}
        for cp in cps.values():
            cp.start()
        for k in (1, -1):
            yield t0 + HOP
            cps[k].wait_recv()
            done(-k, t0 + HOP)
        more = {}
        for k in (1, -1):
            t = t0 + HOP + 0.5
            yield t
            b = mod(y - 2 * k, NY)
            more[k] = [wcopy(view(b), (y_up, y_dn)[k < 0]), wcopy(half(b, k), (y_up2, y_dn2)[k < 0])]
            cps[2 * k].wait_recv()
            for cp in more[k]:
                cp.start()
            done(-2 * k, t)
        for k in (1, -1):
            t = t0 + 2 * HOP + 0.5
            yield t
            more[k][0].wait_recv()
            done(-3 * k, t)
        t = t0 + 2 * HOP + 1
        yield t
        more[1][1].wait_recv()
        more[-1][1].wait_recv()
        done(4, t)

    a_rows, b_rows = pl.ds(0, WA), pl.ds(WA, PIECE - WA)

    def spread_ay(delta, t):
        b = mod(x + delta, NX)
        put(track(spread(NY, y, y_up, y_dn, lambda k: wbuf.at[b, k, a_rows],
                         lambda k, sign: wbuf.at[b, k, pl.ds(0 if sign > 0 else 16, 16)], nothing, t)), t)

    def spread_bx(delta, t):
        b = mod(y + delta, NY)

        def half(k, sign):
            if (sign > 0) == (delta % 2 == 0):
                return wbuf.at[k, b, pl.ds(WA, 32)]
            return wbuf.at[k, b, pl.ds(WA + 32, 16)]

        put(track(spread(NX, x, x_up, x_dn, lambda k: wbuf.at[k, b, b_rows], half, nothing, t)), t)

    def weights():
        @pl.when(is_src)
        def _():
            wlocal.wait()

        @pl.when(jnp.logical_not(is_src))
        def _():
            wcp[0].wait_recv()

        put(track(spread_x(lambda b: wbuf.at[b, y, a_rows], spread_ay, W0)), W0)
        put(track(spread_y(lambda b: wbuf.at[x, b, b_rows],
                           lambda b, sign: wbuf.at[x, b, pl.ds(WA, 32) if sign > 0 else pl.ds(WA + 32, 16)], spread_bx, W0)), W0)
        spread_ay(0, W0)
        spread_bx(0, W0)
        yield W0

    def send_ctx():
        for cp in zctxb_cp + zctxa_cp:
            cp.start()
        yield 0

    W0 = 8.0
    put(weights(), W0)
    put(send_ctx(), 9.0)

    load_cot.wait()
    fill_cot(pcot, 1 - c, 0)
    core_send(pcot, kcot, 0, 1)
    fill_ctx(pctx, 1 - c, 0, 0)
    fill_ctx(pctx, 1 - c, 0, 1)
    core_send(pctxa, kctxa, 0, 1)
    core_send(pctxb, kctxb, 0, 1)
    fill_cot(kcot, c, 0)
    fill_ctx(kctx, c, 0, 0)
    fill_ctx(kctx, c, 0, 1)
    run(15.0)
    for cp in zcot_cp:
        cp.wait_recv()
    for slot in (1, 2):
        fill_cot(pcot, 1 - c, slot)
    core_send(pcot, kcot, 1, 3)
    for slot in (1, 2):
        fill_cot(kcot, c, slot)

    taken = [0]

    def terms(part, cps, t0):
        run(t0)
        for cp in cps:
            cp.wait_recv()
        for slot in (1, 2):
            fill_ctx(pctx, 1 - c, slot, part)
        core_send(pctx[part], kctx[part], 1, 3)
        for slot in (1, 2):
            fill_ctx(kctx, c, slot, part)
        for cp in own_core[taken[0]:]:
            cp.wait_recv()
        taken[0] = len(own_core)
        for kk in range(2):
            @pl.loop(0, C // 256)
            def _(i):
                rows = pl.ds(pl.multiple_of(i * 256, 256), 256)
                t[part][kk, rows, :] = lax.dot_general(kcot[kk, :, rows], kctx[part][kk], (((0,), (0,)), ((), ())),
                                                       preferred_element_type=jnp.float32)

    gn = [0]

    def gcopy(src, dst, to):
        i = gn[0]
        gn[0] += 1
        cp = rc(src, dst, gs.at[i], gr.at[i], to)
        pending.append(cp)
        cp.start()
        return cp

    def rows_of(xb, yb):
        return pl.ds(pl.multiple_of((xb * NY + yb) * ROWS, 8), ROWS)

    class Chains:
        def __init__(self, n, me, d, to, slot):
            self.n, self.me, self.d, self.to, self.slot = n, me, d, to, slot
            self.last = {1: None, -1: None}

        @staticmethod
        def deltas(n):
            out = [n // 2]
            for k in range(n // 2 - 1, 0, -1):
                out += [-k, k]
            return out + [0]

        def step(self, k, own):
            half = self.n // 2
            if k == 0:
                for way in (1, -1):
                    self.last[way].wait_recv()
                res = self.slot(1, half - 1)
                res[...] = own[...] + res[...] + self.slot(-1, half - 2)[...]
                return res
            way = 1 if k > 0 else -1
            length = half if way > 0 else half - 1
            s = length - abs(k)
            src = own
            if s > 0:
                self.last[way].wait_recv()
                src = self.slot(way, s - 1)
                src[...] = src[...] + own[...]
            self.last[way] = gcopy(src, self.slot(way, s), self.to[way * self.d])
            return None

    x_to, y_to = {1: x_up, -1: x_dn}, {1: y_up, -1: y_dn}

    def slots(ref, half):
        return lambda way, s: ref.at[s if way > 0 else half + s]

    base = 23.0

    def finish(kk, got, part):
        layer = zp + 4 * c + 2 * kk
        for cc in range(2):
            here = got.at[pl.ds(16 * cc, WIN)]
            there = fr[part].at[zh]
            i = 4 * part + 2 * kk + cc
            send = rc(here, there, ls.at[i], lr.at[4 * part + zh], dev(cc=cc, zz=layer))
            same = jnp.logical_and(layer == z, c == cc)
            last.append((send, same))

            @pl.when(jnp.logical_not(same))
            def _():
                send.start()

            @pl.when(same)
            def _():
                there[...] = here[...]

    last = []

    def chain_a(kk, j, second):
        d = 1 - 2 * kk
        k2 = Chains.deltas(NX)[j]
        q = mod(x + d * k2, NX)
        ring = Chains(NY, y, d, y_to, slots(ray.at[kk, j], NY // 2))
        t0 = base + 3.0 + 4.5 * j
        for i, k in enumerate(Chains.deltas(NY)):
            got = ring.step(k, ta.at[kk, rows_of(q, mod(y + d * k, NY))])
            if k < 0 or k == 1:
                yield t0 + 3.6 * (i // 2 + 1)
        got = second.step(k2, got)
        if k2 == 0:
            finish(kk, got, 0)

    def chain_b(kk, j, second):
        d = 1 - 2 * kk
        k2 = Chains.deltas(NY)[j]
        q = mod(y + d * k2, NY)
        ring = Chains(NX, x, d, x_to, slots(rbx.at[kk, j], NX // 2))
        t0 = base + 3.7 * j
        for i, k in enumerate(Chains.deltas(NX)):
            got = ring.step(k, tb.at[kk, rows_of(mod(x + d * k, NX), q)])
            if k == -1:
                yield t0 + 4.5
            elif k == 1:
                yield t0 + 8.5
        got = second.step(k2, got)
        if k2 == 0:
            finish(kk, got, 1)

    a_second = [Chains(NX, x, 1 - 2 * kk, x_to, slots(rax.at[kk], NX // 2)) for kk in range(2)]
    b_second = [Chains(NY, y, 1 - 2 * kk, y_to, slots(rby.at[kk], NY // 2)) for kk in range(2)]
    for j in range(8):
        for kk in range(2):
            put(chain_b(kk, j, b_second[kk]), base + max(0, 3.7 * (j - 1)))
    for j in range(4):
        for kk in range(2):
            put(chain_a(kk, j, a_second[kk]), base + 3.0 + max(0, 5.7 * (j - 2)))
    terms(1, zctxb_cp, 19.0)
    run(base + 0.1)
    terms(0, zctxa_cp, base + 0.2)
    run(base + 3.1)

    def outputs():
        late = 0
        while spreading[0]:
            late += 1
            yield base + 6 + late
        for kk in range(2):
            @pl.loop(0, 3)
            def _(i):
                rows = pl.ds(pl.multiple_of(i * FR, FR), FR)
                fall[2 * c + kk, rows, :] = jnp.dot(kcot[kk, rows, :], wbuf[pl.ds(2 * kk, 2)].reshape(C, HW),
                                                    preferred_element_type=jnp.float32).astype(jnp.bfloat16)
                more = pl.ds(pl.multiple_of(KS + i * FR, FR), FR)
                fs[kk, rows, :] = jnp.dot(kcot[kk, more, :], wbuf[pl.ds(2 * kk, 2)].reshape(C, HW),
                                          preferred_element_type=jnp.float32).astype(jnp.bfloat16)
            if kk == 0:
                yield base + 9
        back = rc(fs, fall.at[pl.ds(2 * c, 2)], fs_s.at[0], fs_r.at[0], sib)
        back.start()
        pending.append(back)
        yield base + 14
        back.wait_recv()
        for u in (0, 1):
            rbl[u] = fall[host_of(zl, u) >> 1, FR:2 * FR, :]
            rbr[u] = fall[host_of(zrr, u + 2) >> 1, 2 * FR:3 * FR, :]
        to_dn = rc(rbl, rrr, fs_s.at[1], fs_r.at[1], z_dn)
        to_up = rc(rbr, rrl, fs_s.at[2], fs_r.at[2], z_up)
        to_dn.start()
        to_up.start()
        pending.extend((to_dn, to_up))
        yield base + 26
        to_dn.wait_recv()
        to_up.wait_recv()
        for u in range(UD):
            h = host_of(z, u)
            mine = jnp.full((FR, HW), h & 1, jnp.int32) == zp
            got = rrr[u] if u < 2 else rrl[u - 2]
            val = jnp.where(mine, fall[h >> 1, 0:FR, :], got)
            fg_ref[u] = jnp.where(frame < counts[u], val, jnp.zeros((FR, HW), jnp.bfloat16))

    put(outputs(), base + 6)
    run(base + 1000)

    for part in range(2):
        for i in range(4):
            got = rc(fr[part].at[i], fr[part].at[i], ls.at[0], lr.at[4 * part + i], sib)

            @pl.when(jnp.logical_not(jnp.logical_and(zh == i, z // 4 == c)))
            def _():
                got.wait_recv()
    for part, cols in ((0, slice(0, CUT)), (1, slice(CUT, HW))):
        ref = fr[part]
        first = ref[0, 0:20, :] + ref[1, 0:20, :] + ref[2, 0:20, :] + ref[3, 0:20, :]
        second = ref[0, 4:24, :] + ref[1, 4:24, :] + ref[2, 4:24, :] + ref[3, 4:24, :]
        wg_ref[:, cols] = jnp.where(jnp.full(first.shape, c, jnp.int32) == 0, first, second).astype(jnp.bfloat16)

    for send, same in last:
        @pl.when(jnp.logical_not(same))
        def _():
            send.wait_send()

    for cp in zcot_cp + zctxa_cp + zctxb_cp + own_core + pending:
        cp.wait_send()

    @pl.when(is_src)
    def _():
        for cp in wcp:
            cp.wait_send()


def local(saved_context, cotangent, out_proj, frame_counts, host_segment):
    bf, f32, dma = jnp.bfloat16, jnp.float32, pltpu.SemaphoreType.DMA
    smem, vmem, hbm = (pl.BlockSpec(memory_space=m) for m in (pltpu.SMEM, pltpu.VMEM, pl.ANY))
    fg, wg = pl.pallas_call(
        kernel,
        name="backward",
        out_shape=(jax.ShapeDtypeStruct((UD, FR, HW), bf), jax.ShapeDtypeStruct((20, HW), bf)),
        in_specs=[smem, smem, hbm, hbm, hbm],
        out_specs=(vmem, vmem),
        scratch_shapes=[
            pltpu.VMEM((UD, FR, HW), bf),
            pltpu.VMEM((UD, FR, C), bf),
            pltpu.VMEM((UD, FR, CUT), bf),
            pltpu.VMEM((UD, FR, HW - CUT), bf),
            pltpu.VMEM((4, FR, C), bf),
            pltpu.VMEM((2, 2 * KS, CUT), bf),
            pltpu.VMEM((2, 2 * KS, HW - CUT), bf),
            pltpu.VMEM((2, 2 * KS, C), bf),
            pltpu.VMEM((2, KS, CUT), bf),
            pltpu.VMEM((2, KS, HW - CUT), bf),
            pltpu.VMEM((2, KS, C), bf),
            pltpu.VMEM((NX, NY, PIECE, HW), bf),
            pltpu.VMEM((2, C, CUT), f32),
            pltpu.VMEM((2, C, HW - CUT), f32),
            pltpu.VMEM((2, NX, NY - 1, ROWS, CUT), f32),
            pltpu.VMEM((2, NX - 1, ROWS, CUT), f32),
            pltpu.VMEM((2, NY, NX - 1, ROWS, HW - CUT), f32),
            pltpu.VMEM((2, NY - 1, ROWS, HW - CUT), f32),
            pltpu.VMEM((4, WIN, CUT), f32),
            pltpu.VMEM((4, WIN, HW - CUT), f32),
            pltpu.VMEM((4, KS, HW), bf),
            pltpu.VMEM((2, KS, HW), bf),
            pltpu.VMEM((2, FR, HW), bf),
            pltpu.VMEM((2, FR, HW), bf),
            pltpu.VMEM((2, FR, HW), bf),
            pltpu.VMEM((2, FR, HW), bf),
            dma((3,)),
            dma((16,)), dma((16,)),
            dma((12,)), dma((12,)),
            dma((80,)), dma((80,)),
            dma((128,)), dma((128,)),
            dma((3,)), dma((3,)),
            dma((8,)), dma((8,)),
        ],
        compiler_params=pltpu.CompilerParams(collective_id=0, has_side_effects=True, vmem_limit_bytes=56 << 20),
    )(host_segment, frame_counts, saved_context, cotangent, out_proj[0])
    return fg, wg[None]


def solution(mesh):
    placed = (
        P(("dp", "segment"), None, None),
        P(("dp", "segment"), None, None),
        P("segment", None, None),
        P(("dp", "segment")),
        P("dp"),
    )
    return jax.shard_map(
        local,
        mesh=mesh,
        in_specs=placed,
        out_specs=(P(("dp", "segment"), None, None), P("segment", "dp", None)),
        check_vma=False,
    )
```

```python
import functools
import heapq

import jax
import jax.numpy as jnp
from jax import lax
from jax.experimental import pallas as pl
from jax.experimental.pallas import tpu as pltpu
from jax.sharding import PartitionSpec as P

MESH = pl.DeviceIdType.MESH
NX, NY, NC, NZ = 4, 8, 2, 8
C, HW, FR, UD = 1280, 640, 128, 4
LAYERS = 8
KS = 4 * FR
CUT = 256
PIECE = C * 2 // (NX * NY)
WA = 32
ROWS = C // (NX * NY)
WIN = 24


def kernel(host, counts, ctx, cot, w, fg_ref, wg_ref, uctx, ucot, pctxa, pctxb, pcot, kctxa, kctxb, kcot, wbuf, ta, tb, ray, rax, rbx,
           rby, fra, frb, fs, ret, lsem, us, ur, ws, wr, gs, gr, bs, br, ls, lr):
    kctx, pctx, t, fr = (kctxa, kctxb), (pctxa, pctxb), (ta, tb), (fra, frb)
    dp = lax.axis_index("dp")
    z = lax.axis_index("segment")
    x, y, c = dp // (NY * NC), lax.rem(dp // NC, NY), lax.rem(dp, NC)
    zp, zh = lax.rem(z, 2), z // 2

    def dev(xx=None, yy=None, cc=None, zz=None):
        xx, yy, cc, zz = (b if a is None else a for a, b in ((xx, x), (yy, y), (cc, c), (zz, z)))
        return ((xx * NY + yy) * NC + cc, zz)

    def mod(v, n):
        return lax.rem(v + 2 * n, n)

    z_up, z_dn = mod(z + 1, NZ), mod(z - 1, NZ)
    x_up, x_dn = dev(xx=mod(x + 1, NX)), dev(xx=mod(x - 1, NX))
    y_up, y_dn = dev(yy=mod(y + 1, NY)), dev(yy=mod(y - 1, NY))
    sib = dev(cc=1 - c)

    bar = pltpu.get_barrier_semaphore()
    x_far, y_up2, y_dn2 = dev(xx=mod(x + 2, NX)), dev(yy=mod(y + 2, NY)), dev(yy=mod(y - 2, NY))
    partners = [x_up, x_dn, y_up, y_dn, sib, x_far, y_up2, y_dn2]
    for d in (1, 2, 4, 6, 7):
        for cc in (c, 1 - c):
            partners.append(dev(cc=cc, zz=mod(z + d, NZ)))
    for p in partners:
        pl.semaphore_signal(bar, inc=1, device_id=p, device_id_type=MESH)

    load_ctx = pltpu.make_async_copy(ctx, uctx, lsem.at[0])
    load_cot = pltpu.make_async_copy(cot, ucot, lsem.at[1])
    load_ctx.start()
    load_cot.start()

    load_ctx.wait()
    load_cot.wait()
    frame = lax.broadcasted_iota(jnp.int32, (FR, HW), 0)

    def pack(layer):
        idx, valid = jnp.int32(0), jnp.int32(0)
        for u in range(UD):
            mine = host[z * UD + u] == layer
            idx = jnp.where(mine, jnp.int32(u), idx)
            valid = jnp.where(mine, jnp.int32(1), valid)
        pcot[layer] = ucot[idx]
        val = jnp.where(frame < counts[idx] * valid, uctx[idx], jnp.zeros((FR, HW), jnp.bfloat16))
        pctxa[layer] = val[:, 0:CUT]
        pctxb[layer] = val[:, CUT:HW]

    away = [[1 - zp + 4 * cc + 2 * kk for cc in range(2)] for kk in range(2)]
    for kk in range(2):
        for cc in range(2):
            pack(away[kk][cc])
    pl.semaphore_wait(bar, len(partners))

    def rc(src, dst, ssem, rsem, to):
        return pltpu.make_async_remote_copy(src_ref=src, dst_ref=dst, send_sem=ssem, recv_sem=rsem, device_id=to, device_id_type=MESH)

    kkp, row0 = x // 2, lax.rem(x, 2) * (C // 2) + y * PIECE
    wsrc = w.at[pl.ds(pl.multiple_of(row0, 16), PIECE)]
    wdst = wbuf.at[x, y]
    is_src = zh == 2 * c + kkp
    wcp = [rc(wsrc, wdst, ws.at[i], wr.at[0], dev(zz=mod(z + d, NZ))) for i, d in enumerate((2, 4, 6))]
    wlocal = pltpu.make_async_copy(wsrc, wdst, lsem.at[2])

    @pl.when(is_src)
    def _():
        for cp in wcp:
            cp.start()
        wlocal.start()

    def place(p):
        return pl.ds(pl.multiple_of(p * FR, FR), FR)

    nu = [0]

    def ucopy(src, dst, rsem, to):
        i = nu[0]
        nu[0] += 1
        cp = rc(src, dst, us.at[i], ur.at[rsem], to)
        pending.append(cp)
        return cp

    pending = []
    half = FR // 2
    z_cot, z_ctx = [], ([], [])
    for kk in range(2):
        for cc in range(2):
            to = dev(cc=cc, zz=(z_up, z_dn)[kk])
            layer = away[kk][cc]
            for h in range(2):
                rows = pl.ds(pl.multiple_of((2 + c) * FR + h * half, half), half)
                z_cot.append(ucopy(pcot.at[layer, pl.ds(h * half, half)], kcot.at[kk, rows], 4 * kk + 2 * h + c, to))
            for part in range(2):
                z_ctx[part].append(ucopy(pctx[part].at[layer], kctx[part].at[kk, place(2 + c)], 8 + 4 * part + 2 * kk + c, to))
    for cp in z_cot:
        cp.start()
    near = []
    for kk in range(2):
        layer = zp + 4 * (1 - c) + 2 * kk
        pack(layer)
        near.append(ucopy(pcot.at[layer], kcot.at[kk, place(c)], 16 + kk, sib))
        for part in range(2):
            near.append(ucopy(pctx[part].at[layer], kctx[part].at[kk, place(c)], 18 + 2 * part + kk, sib))
    for cp in near:
        cp.start()
    for kk in range(2):
        layer = zp + 4 * c + 2 * kk
        pack(layer)
        kcot[kk, place(c), :] = pcot[layer]
        for part in range(2):
            kctx[part][kk, place(c), :] = pctx[part][layer]

    queue = []
    order = [0]

    def put(gen, when):
        heapq.heappush(queue, (when, order[0], gen))
        order[0] += 1

    def run(until):
        while queue and queue[0][0] < until:
            _, _, gen = heapq.heappop(queue)
            try:
                put(gen, next(gen))
            except StopIteration:
                pass

    wn = [3]

    spreading = [0]

    def track(gen):
        spreading[0] += 1
        yield from gen
        spreading[0] -= 1

    def wcopy(ref, to):
        i = wn[0]
        wn[0] += 1
        cp = rc(ref, ref, ws.at[i], wr.at[i], to)
        pending.append(cp)
        return cp

    HOP = 3.0

    def spread(n, me, up, dn, view, half, done, t0):
        far = n // 2
        ups, dns = [wcopy(view(me), up)], [wcopy(view(me), dn)]
        ups[0].start()
        dns[0].start()
        for s in range(1, far):
            for lst, to, sign in ((ups, up, 1), (dns, dn, -1)):
                t = t0 + HOP * s
                yield t
                ref = view(mod(me - sign * s, n))
                if s == far - 1:
                    ref = half(mod(me - sign * s, n), sign)
                cp = wcopy(ref, to)
                lst[-1].wait_recv()
                cp.start()
                lst.append(cp)
                done(-sign * s, t)
        t = t0 + HOP * far
        yield t
        ups[-1].wait_recv()
        dns[-1].wait_recv()
        done(far, t)

    def nothing(delta, t):
        pass

    def spread_x(view, done, t0):
        cps = [wcopy(view(x), to) for to in (x_up, x_dn, x_far)]
        for cp in cps:
            cp.start()
        for cp, delta in zip(cps, (-1, 1, 2)):
            yield t0 + HOP
            cp.wait_recv()
            done(delta, t0 + HOP)

    def spread_y(view, half, done, t0):
        cps = {k: wcopy(view(y), to) for k, to in ((1, y_up), (-1, y_dn), (2, y_up2), (-2, y_dn2))}
        for cp in cps.values():
            cp.start()
        for k in (1, -1):
            yield t0 + HOP
            cps[k].wait_recv()
            done(-k, t0 + HOP)
        more = {}
        for k in (1, -1):
            t = t0 + HOP + 0.5
            yield t
            b = mod(y - 2 * k, NY)
            more[k] = [wcopy(view(b), (y_up, y_dn)[k < 0]), wcopy(half(b, k), (y_up2, y_dn2)[k < 0])]
            cps[2 * k].wait_recv()
            for cp in more[k]:
                cp.start()
            done(-2 * k, t)
        for k in (1, -1):
            t = t0 + 2 * HOP + 0.5
            yield t
            more[k][0].wait_recv()
            done(-3 * k, t)
        t = t0 + 2 * HOP + 1
        yield t
        more[1][1].wait_recv()
        more[-1][1].wait_recv()
        done(4, t)

    a_rows, b_rows = pl.ds(0, WA), pl.ds(WA, PIECE - WA)

    def spread_ay(delta, t):
        b = mod(x + delta, NX)
        put(track(spread(NY, y, y_up, y_dn, lambda k: wbuf.at[b, k, a_rows],
                         lambda k, sign: wbuf.at[b, k, pl.ds(0 if sign > 0 else 16, 16)], nothing, t)), t)

    def spread_bx(delta, t):
        b = mod(y + delta, NY)

        def half(k, sign):
            if (sign > 0) == (delta % 2 == 0):
                return wbuf.at[k, b, pl.ds(WA, 32)]
            return wbuf.at[k, b, pl.ds(WA + 32, 16)]

        put(track(spread(NX, x, x_up, x_dn, lambda k: wbuf.at[k, b, b_rows], half, nothing, t)), t)

    def weights():
        @pl.when(is_src)
        def _():
            wlocal.wait()

        @pl.when(jnp.logical_not(is_src))
        def _():
            wcp[0].wait_recv()

        put(track(spread_x(lambda b: wbuf.at[b, y, a_rows], spread_ay, W0)), W0)
        put(track(spread_y(lambda b: wbuf.at[x, b, b_rows],
                           lambda b, sign: wbuf.at[x, b, pl.ds(WA, 32) if sign > 0 else pl.ds(WA + 32, 16)], spread_bx, W0)), W0)
        spread_ay(0, W0)
        spread_bx(0, W0)
        yield W0

    def send_ctx():
        for cp in z_ctx[1] + z_ctx[0]:
            cp.start()
        yield 0

    W0 = 6.0
    put(weights(), W0)
    put(send_ctx(), 9.0)

    def ready(part, t0):
        run(t0)
        for cp in near[1 + part::3]:
            cp.wait_recv()
        if part == 1:
            for cp in near[0::3]:
                cp.wait_recv()
        for kk in range(2):
            for src in range(2):
                if part == 1:
                    for h in range(2):
                        rows = pl.ds((2 + src) * FR + h * half, half)
                        rc(pcot.at[0, pl.ds(0, half)], kcot.at[kk, rows], us.at[0], ur.at[4 * kk + 2 * h + src], sib).wait_recv()
                there = kctx[part].at[kk, pl.ds((2 + src) * FR, FR)]
                rc(pctx[part].at[0], there, us.at[0], ur.at[8 + 4 * part + 2 * kk + src], sib).wait_recv()

    def terms(part, kk):
        @pl.loop(0, C // 256)
        def _(i):
            rows = pl.ds(pl.multiple_of(i * 256, 256), 256)
            t[part][kk, rows, :] = lax.dot_general(kcot[kk, :, rows], kctx[part][kk], (((0,), (0,)), ((), ())),
                                                   preferred_element_type=jnp.float32)

    gn = [0]

    def gcopy(src, dst, to):
        i = gn[0]
        gn[0] += 1
        cp = rc(src, dst, gs.at[i], gr.at[i], to)
        pending.append(cp)
        cp.start()
        return cp

    def rows_of(xb, yb):
        return pl.ds(pl.multiple_of((xb * NY + yb) * ROWS, 8), ROWS)

    class Chains:
        def __init__(self, n, me, d, to, slot):
            self.n, self.me, self.d, self.to, self.slot = n, me, d, to, slot
            self.last = {1: None, -1: None}

        @staticmethod
        def deltas(n):
            out = [n // 2]
            for k in range(n // 2 - 1, 0, -1):
                out += [-k, k]
            return out + [0]

        def step(self, k, own):
            half = self.n // 2
            if k == 0:
                for way in (1, -1):
                    self.last[way].wait_recv()
                res = self.slot(1, half - 1)
                res[...] = own[...] + res[...] + self.slot(-1, half - 2)[...]
                return res
            way = 1 if k > 0 else -1
            length = half if way > 0 else half - 1
            s = length - abs(k)
            src = own
            if s > 0:
                self.last[way].wait_recv()
                src = self.slot(way, s - 1)
                src[...] = src[...] + own[...]
            self.last[way] = gcopy(src, self.slot(way, s), self.to[way * self.d])
            return None

    x_to, y_to = {1: x_up, -1: x_dn}, {1: y_up, -1: y_dn}

    def slots(ref, half):
        return lambda way, s: ref.at[s if way > 0 else half + s]

    base = 23.0

    def finish(kk, got, part):
        layer = zp + 4 * c + 2 * kk
        for cc in range(2):
            here = got.at[pl.ds(16 * cc, WIN)]
            there = fr[part].at[zh]
            i = 4 * part + 2 * kk + cc
            send = rc(here, there, ls.at[i], lr.at[4 * part + zh], dev(cc=cc, zz=layer))
            same = jnp.logical_and(layer == z, c == cc)
            last.append((send, same))

            @pl.when(jnp.logical_not(same))
            def _():
                send.start()

            @pl.when(same)
            def _():
                there[...] = here[...]

    last = []

    def chain_a(kk, j, second):
        d = 1 - 2 * kk
        k2 = Chains.deltas(NX)[j]
        q = mod(x + d * k2, NX)
        ring = Chains(NY, y, d, y_to, slots(ray.at[kk, j], NY // 2))
        t0 = base + 3.0 + 4.5 * j
        for i, k in enumerate(Chains.deltas(NY)):
            got = ring.step(k, ta.at[kk, rows_of(q, mod(y + d * k, NY))])
            if k < 0 or k == 1:
                yield t0 + 3.6 * (i // 2 + 1)
        got = second.step(k2, got)
        if k2 == 0:
            finish(kk, got, 0)

    def chain_b(kk, j, second):
        d = 1 - 2 * kk
        k2 = Chains.deltas(NY)[j]
        q = mod(y + d * k2, NY)
        ring = Chains(NX, x, d, x_to, slots(rbx.at[kk, j], NX // 2))
        t0 = base + 3.7 * j
        for i, k in enumerate(Chains.deltas(NX)):
            got = ring.step(k, tb.at[kk, rows_of(mod(x + d * k, NX), q)])
            if k == -1:
                yield t0 + 4.5
            elif k == 1:
                yield t0 + 8.5
        got = second.step(k2, got)
        if k2 == 0:
            finish(kk, got, 1)

    a_second = [Chains(NX, x, 1 - 2 * kk, x_to, slots(rax.at[kk], NX // 2)) for kk in range(2)]
    b_second = [Chains(NY, y, 1 - 2 * kk, y_to, slots(rby.at[kk], NY // 2)) for kk in range(2)]
    for j in range(8):
        for kk in range(2):
            put(chain_b(kk, j, b_second[kk]), base + 0.1 * kk + max(0, 3.7 * (j - 1)))
    for j in range(4):
        for kk in range(2):
            put(chain_a(kk, j, a_second[kk]), base + 3.0 + 0.1 * kk + max(0, 5.7 * (j - 2)))
    ready(1, 19.0)
    terms(1, 0)
    run(base + 0.05)
    terms(1, 1)
    run(base + 0.15)
    ready(0, base + 0.2)
    terms(0, 0)
    run(base + 3.05)
    terms(0, 1)
    run(base + 3.15)

    def outputs():
        now = base + 6
        while spreading[0]:
            now += 1
            yield now
        back = []
        for kk in range(2):
            layer = zp + 4 * c + 2 * kk

            @pl.loop(0, 4)
            def _(i):
                fs[kk, place(i), :] = jnp.dot(kcot[kk, place(i), :], wbuf[pl.ds(2 * kk, 2)].reshape(C, HW),
                                              preferred_element_type=jnp.float32).astype(jnp.bfloat16)
            for p, to in ((2, dev(cc=0, zz=(z_dn, z_up)[kk])), (3, dev(cc=1, zz=(z_dn, z_up)[kk])), (1 - c, sib)):
                back.append(rc(fs.at[kk, place(p)], ret.at[layer], bs.at[len(back)], br.at[layer], to))
                back[-1].start()
            ret[layer] = fs[kk, place(c), :]
            if kk == 0:
                now += 3
                yield now
        pending.extend(back)
        yield now + 15
        for kk in range(2):
            for layer in (zp + 4 * (1 - c) + 2 * kk, away[kk][0], away[kk][1]):
                rc(fs.at[kk, place(0)], ret.at[layer], bs.at[0], br.at[layer], sib).wait_recv()
        for u in range(UD):
            fg_ref[u] = jnp.where(frame < counts[u], ret[host[z * UD + u]], jnp.zeros((FR, HW), jnp.bfloat16))

    put(outputs(), base + 6)
    run(base + 1000)

    for part in range(2):
        for i in range(4):
            got = rc(fr[part].at[i], fr[part].at[i], ls.at[0], lr.at[4 * part + i], sib)

            @pl.when(jnp.logical_not(jnp.logical_and(zh == i, z // 4 == c)))
            def _():
                got.wait_recv()
    for part, cols in ((0, slice(0, CUT)), (1, slice(CUT, HW))):
        ref = fr[part]
        first = ref[0, 0:20, :] + ref[1, 0:20, :] + ref[2, 0:20, :] + ref[3, 0:20, :]
        second = ref[0, 4:24, :] + ref[1, 4:24, :] + ref[2, 4:24, :] + ref[3, 4:24, :]
        wg_ref[:, cols] = jnp.where(jnp.full(first.shape, c, jnp.int32) == 0, first, second).astype(jnp.bfloat16)

    for send, same in last:
        @pl.when(jnp.logical_not(same))
        def _():
            send.wait_send()

    for cp in pending:
        cp.wait_send()

    @pl.when(is_src)
    def _():
        for cp in wcp:
            cp.wait_send()


def local(saved_context, cotangent, out_proj, frame_counts, host_segment):
    bf, f32, dma = jnp.bfloat16, jnp.float32, pltpu.SemaphoreType.DMA
    smem, vmem, hbm = (pl.BlockSpec(memory_space=m) for m in (pltpu.SMEM, pltpu.VMEM, pl.ANY))
    fg, wg = pl.pallas_call(
        kernel,
        name="backward",
        out_shape=(jax.ShapeDtypeStruct((UD, FR, HW), bf), jax.ShapeDtypeStruct((20, HW), bf)),
        in_specs=[smem, smem, hbm, hbm, hbm],
        out_specs=(vmem, vmem),
        scratch_shapes=[
            pltpu.VMEM((UD, FR, HW), bf),
            pltpu.VMEM((UD, FR, C), bf),
            pltpu.VMEM((LAYERS, FR, CUT), bf),
            pltpu.VMEM((LAYERS, FR, HW - CUT), bf),
            pltpu.VMEM((LAYERS, FR, C), bf),
            pltpu.VMEM((2, KS, CUT), bf),
            pltpu.VMEM((2, KS, HW - CUT), bf),
            pltpu.VMEM((2, KS, C), bf),
            pltpu.VMEM((NX, NY, PIECE, HW), bf),
            pltpu.VMEM((2, C, CUT), f32),
            pltpu.VMEM((2, C, HW - CUT), f32),
            pltpu.VMEM((2, NX, NY - 1, ROWS, CUT), f32),
            pltpu.VMEM((2, NX - 1, ROWS, CUT), f32),
            pltpu.VMEM((2, NY, NX - 1, ROWS, HW - CUT), f32),
            pltpu.VMEM((2, NY - 1, ROWS, HW - CUT), f32),
            pltpu.VMEM((4, WIN, CUT), f32),
            pltpu.VMEM((4, WIN, HW - CUT), f32),
            pltpu.VMEM((2, KS, HW), bf),
            pltpu.VMEM((LAYERS, FR, HW), bf),
            dma((3,)),
            dma((24,)), dma((24,)),
            dma((80,)), dma((80,)),
            dma((128,)), dma((128,)),
            dma((8,)), dma((8,)),
            dma((8,)), dma((8,)),
        ],
        compiler_params=pltpu.CompilerParams(collective_id=0, has_side_effects=True, vmem_limit_bytes=56 << 20),
    )(host_segment, frame_counts, saved_context, cotangent, out_proj[0])
    return fg, wg[None]


def solution(mesh):
    placed = (
        P(("dp", "segment"), None, None),
        P(("dp", "segment"), None, None),
        P("segment", None, None),
        P(("dp", "segment")),
        P("dp"),
    )
    return jax.shard_map(
        local,
        mesh=mesh,
        in_specs=placed,
        out_specs=(P(("dp", "segment"), None, None), P("segment", "dp", None)),
        check_vma=False,
    )
```

```python
import functools
import heapq

import jax
import jax.numpy as jnp
from jax import lax
from jax.experimental import pallas as pl
from jax.experimental.pallas import tpu as pltpu
from jax.sharding import PartitionSpec as P

MESH = pl.DeviceIdType.MESH
NX, NY, NC, NZ = 4, 8, 2, 8
C, HW, FR, UD = 1280, 640, 128, 4
LAYERS = 8
KS = 4 * FR
CUT = 256
PIECE = C * 2 // (NX * NY)
WA = 32
WB = 64
ROWS = C // (NX * NY)
WIN = 24


def kernel(host, counts, ctx, cot, w, fg_ref, wg_ref, uctx, ucot, pctxa, pctxb, pcot, kctxa, kctxb, kcot, wbuf, ta, tb, ray, rax, rbx,
           rby, fra, frb, fs, ret, fgv, lsem, us, ur, ws, wr, gs, gr, bs, br, ls, lr):
    kctx, pctx, t, fr = (kctxa, kctxb), (pctxa, pctxb), (ta, tb), (fra, frb)
    dp = lax.axis_index("dp")
    z = lax.axis_index("segment")
    x, y, c = dp // (NY * NC), lax.rem(dp // NC, NY), lax.rem(dp, NC)
    zp, zh = lax.rem(z, 2), z // 2

    def dev(xx=None, yy=None, cc=None, zz=None):
        xx, yy, cc, zz = (b if a is None else a for a, b in ((xx, x), (yy, y), (cc, c), (zz, z)))
        return ((xx * NY + yy) * NC + cc, zz)

    def mod(v, n):
        return lax.rem(v + 2 * n, n)

    z_up, z_dn = mod(z + 1, NZ), mod(z - 1, NZ)
    x_up, x_dn = dev(xx=mod(x + 1, NX)), dev(xx=mod(x - 1, NX))
    y_up, y_dn = dev(yy=mod(y + 1, NY)), dev(yy=mod(y - 1, NY))
    sib = dev(cc=1 - c)

    bar = pltpu.get_barrier_semaphore()
    x_far, y_up2, y_dn2 = dev(xx=mod(x + 2, NX)), dev(yy=mod(y + 2, NY)), dev(yy=mod(y - 2, NY))
    partners = [x_up, x_dn, y_up, y_dn, sib, x_far, y_up2, y_dn2]
    for d in (1, 2, 4, 6, 7):
        for cc in (c, 1 - c):
            partners.append(dev(cc=cc, zz=mod(z + d, NZ)))
    for p in partners:
        pl.semaphore_signal(bar, inc=1, device_id=p, device_id_type=MESH)

    load_ctx = pltpu.make_async_copy(ctx, uctx, lsem.at[0])
    load_cot = pltpu.make_async_copy(cot, ucot, lsem.at[1])
    load_ctx.start()
    load_cot.start()

    pl.semaphore_wait(bar, len(partners))

    def rc(src, dst, ssem, rsem, to):
        return pltpu.make_async_remote_copy(src_ref=src, dst_ref=dst, send_sem=ssem, recv_sem=rsem, device_id=to, device_id_type=MESH)

    kkp = x // 2
    wsrc = w.at[lax.rem(x, 2), y, pl.ds(0, WB)]
    wdst = wbuf.at[x, y, pl.ds(0, WB)]
    is_src = zh == 2 * c + kkp
    wcp = [rc(wsrc, wdst, ws.at[i], wr.at[0], dev(zz=mod(z + d, NZ))) for i, d in enumerate((2, 4, 6))]
    wlocal = pltpu.make_async_copy(wsrc, wdst, lsem.at[2])

    @pl.when(is_src)
    def _():
        for cp in wcp:
            cp.start()
        wlocal.start()

    kz, own_core = lax.rem(zh, 2), c == z // 4
    zrows = pl.ds(WB, PIECE - WB)
    wz_src, wz_dst = w.at[:, :, zrows], wbuf.at[pl.ds(2 * kz, 2), :, zrows]
    wz = [rc(wz_src, wz_dst, bs.at[6 + i], br.at[8 + kz], dev(zz=mod(z + d, NZ))) for i, d in enumerate((2, 6, 4))]
    wz_local = pltpu.make_async_copy(wz_src, wz_dst, lsem.at[4])

    def send_rest():
        @pl.when(own_core)
        def _():
            for cp in wz:
                cp.start()
            wz_local.start()
        yield 0

    def rest_there():
        @pl.when(own_core)
        def _():
            wz_local.wait()

        for kk in range(2):
            @pl.when(jnp.logical_not(jnp.logical_and(own_core, kz == kk)))
            def _():
                rc(wz_src, wbuf.at[pl.ds(2 * kk, 2), :, zrows], bs.at[6], br.at[8 + kk], sib).wait_recv()

    load_ctx.wait()
    load_cot.wait()
    frame = lax.broadcasted_iota(jnp.int32, (FR, HW), 0)

    def pack(layer):
        idx, valid = jnp.int32(0), jnp.int32(0)
        for u in range(UD):
            mine = host[z * UD + u] == layer
            idx = jnp.where(mine, jnp.int32(u), idx)
            valid = jnp.where(mine, jnp.int32(1), valid)
        pcot[layer] = ucot[idx]
        val = jnp.where(frame < counts[idx] * valid, uctx[idx], jnp.zeros((FR, HW), jnp.bfloat16))
        pctxa[layer] = val[:, 0:CUT]
        pctxb[layer] = val[:, CUT:HW]

    away = [[1 - zp + 4 * cc + 2 * kk for cc in range(2)] for kk in range(2)]
    for kk in range(2):
        for cc in range(2):
            pack(away[kk][cc])

    def place(p):
        return pl.ds(pl.multiple_of(p * FR, FR), FR)

    nu = [0]

    def ucopy(src, dst, rsem, to):
        i = nu[0]
        nu[0] += 1
        cp = rc(src, dst, us.at[i], ur.at[rsem], to)
        pending.append(cp)
        return cp

    pending = []
    half = FR // 2
    z_cot, z_ctx = [], ([], [])
    for kk in range(2):
        for cc in range(2):
            to = dev(cc=cc, zz=(z_up, z_dn)[kk])
            layer = away[kk][cc]
            for h in range(2):
                rows = pl.ds(pl.multiple_of((2 + c) * FR + h * half, half), half)
                z_cot.append(ucopy(pcot.at[layer, pl.ds(h * half, half)], kcot.at[kk, rows], 4 * kk + 2 * h + c, to))
            for part in range(2):
                z_ctx[part].append(ucopy(pctx[part].at[layer], kctx[part].at[kk, place(2 + c)], 8 + 4 * part + 2 * kk + c, to))
    for cp in z_cot:
        cp.start()
    near = []
    for kk in range(2):
        layer = zp + 4 * (1 - c) + 2 * kk
        pack(layer)
        near.append(ucopy(pcot.at[layer], kcot.at[kk, place(c)], 16 + kk, sib))
        for part in range(2):
            near.append(ucopy(pctx[part].at[layer], kctx[part].at[kk, place(c)], 18 + 2 * part + kk, sib))
    for cp in near:
        cp.start()
    for kk in range(2):
        layer = zp + 4 * c + 2 * kk
        pack(layer)
        kcot[kk, place(c), :] = pcot[layer]
        for part in range(2):
            kctx[part][kk, place(c), :] = pctx[part][layer]

    queue = []
    order = [0]

    def put(gen, when):
        heapq.heappush(queue, (when, order[0], gen))
        order[0] += 1

    def run(until):
        while queue and queue[0][0] < until:
            _, _, gen = heapq.heappop(queue)
            try:
                put(gen, next(gen))
            except StopIteration:
                pass

    wn = [3]

    spreading = [0]

    def track(gen):
        spreading[0] += 1
        yield from gen
        spreading[0] -= 1

    def wcopy(ref, to):
        i = wn[0]
        wn[0] += 1
        cp = rc(ref, ref, ws.at[i], wr.at[i], to)
        pending.append(cp)
        return cp

    HOP = 3.5

    def spread(n, me, up, dn, view, half, done, t0):
        far = n // 2
        ups, dns = [wcopy(view(me), up)], [wcopy(view(me), dn)]
        ups[0].start()
        dns[0].start()
        for s in range(1, far):
            for lst, to, sign in ((ups, up, 1), (dns, dn, -1)):
                t = t0 + HOP * s
                yield t
                ref = view(mod(me - sign * s, n))
                if s == far - 1:
                    ref = half(mod(me - sign * s, n), sign)
                cp = wcopy(ref, to)
                lst[-1].wait_recv()
                cp.start()
                lst.append(cp)
                done(-sign * s, t)
        t = t0 + HOP * far
        yield t
        ups[-1].wait_recv()
        dns[-1].wait_recv()
        done(far, t)

    def nothing(delta, t):
        pass

    def spread_x(view, done, t0):
        cps = [wcopy(view(x), to) for to in (x_up, x_dn, x_far)]
        for cp in cps:
            cp.start()
        for cp, delta in zip(cps, (-1, 1, 2)):
            yield t0 + HOP
            cp.wait_recv()
            done(delta, t0 + HOP)

    def spread_y(view, half, done, t0):
        cps = {k: wcopy(view(y), to) for k, to in ((1, y_up), (-1, y_dn), (2, y_up2), (-2, y_dn2))}
        for cp in cps.values():
            cp.start()
        for k in (1, -1):
            yield t0 + HOP
            cps[k].wait_recv()
            done(-k, t0 + HOP)
        more = {}
        for k in (1, -1):
            t = t0 + HOP + 0.5
            yield t
            b = mod(y - 2 * k, NY)
            more[k] = [wcopy(view(b), (y_up, y_dn)[k < 0]), wcopy(half(b, k), (y_up2, y_dn2)[k < 0])]
            cps[2 * k].wait_recv()
            for cp in more[k]:
                cp.start()
            done(-2 * k, t)
        for k in (1, -1):
            t = t0 + 2 * HOP + 0.5
            yield t
            more[k][0].wait_recv()
            done(-3 * k, t)
        t = t0 + 2 * HOP + 1
        yield t
        more[1][1].wait_recv()
        more[-1][1].wait_recv()
        done(4, t)

    a_rows, b_rows = pl.ds(0, WA), pl.ds(WA, WB - WA)

    def spread_ay(delta, t):
        b = mod(x + delta, NX)
        put(track(spread(NY, y, y_up, y_dn, lambda k: wbuf.at[b, k, a_rows],
                         lambda k, sign: wbuf.at[b, k, pl.ds(0 if sign > 0 else 16, 16)], nothing, t)), t)

    def spread_bx(delta, t):
        b = mod(y + delta, NY)

        put(track(spread(NX, x, x_up, x_dn, lambda k: wbuf.at[k, b, b_rows],
                         lambda k, sign: wbuf.at[k, b, pl.ds(WA if sign > 0 else WA + 16, 16)], nothing, t)), t)

    def weights():
        @pl.when(is_src)
        def _():
            wlocal.wait()

        @pl.when(jnp.logical_not(is_src))
        def _():
            wcp[0].wait_recv()

        put(track(spread_x(lambda b: wbuf.at[b, y, a_rows], spread_ay, W0)), W0)
        put(track(spread_y(lambda b: wbuf.at[x, b, b_rows],
                           lambda b, sign: wbuf.at[x, b, pl.ds(WA if sign > 0 else WA + 16, 16)], spread_bx, W0)), W0)
        spread_ay(0, W0)
        spread_bx(0, W0)
        yield W0

    def send_ctx():
        for cp in z_ctx[1] + z_ctx[0]:
            cp.start()
        yield 0

    W0 = 6.0
    put(weights(), W0)
    put(send_ctx(), 9.0)
    put(send_rest(), 17.0)

    def ready(part, t0):
        run(t0)
        for cp in near[1 + part::3]:
            cp.wait_recv()
        if part == 1:
            for cp in near[0::3]:
                cp.wait_recv()
        for kk in range(2):
            for src in range(2):
                if part == 1:
                    for h in range(2):
                        rows = pl.ds((2 + src) * FR + h * half, half)
                        rc(pcot.at[0, pl.ds(0, half)], kcot.at[kk, rows], us.at[0], ur.at[4 * kk + 2 * h + src], sib).wait_recv()
                there = kctx[part].at[kk, pl.ds((2 + src) * FR, FR)]
                rc(pctx[part].at[0], there, us.at[0], ur.at[8 + 4 * part + 2 * kk + src], sib).wait_recv()

    def terms(part, kk):
        @pl.loop(0, C // 256)
        def _(i):
            rows = pl.ds(pl.multiple_of(i * 256, 256), 256)
            t[part][kk, rows, :] = lax.dot_general(kcot[kk, :, rows], kctx[part][kk], (((0,), (0,)), ((), ())),
                                                   preferred_element_type=jnp.float32)

    gn = [0]

    def gcopy(src, dst, to):
        i = gn[0]
        gn[0] += 1
        cp = rc(src, dst, gs.at[i], gr.at[i], to)
        pending.append(cp)
        cp.start()
        return cp

    def rows_of(xb, yb):
        return pl.ds(pl.multiple_of((xb * NY + yb) * ROWS, 8), ROWS)

    class Chains:
        def __init__(self, n, me, d, to, slot):
            self.n, self.me, self.d, self.to, self.slot = n, me, d, to, slot
            self.last = {1: None, -1: None}

        @staticmethod
        def deltas(n):
            out = [n // 2]
            for k in range(n // 2 - 1, 0, -1):
                out += [-k, k]
            return out + [0]

        def step(self, k, own):
            half = self.n // 2
            if k == 0:
                for way in (1, -1):
                    self.last[way].wait_recv()
                res = self.slot(1, half - 1)
                res[...] = own[...] + res[...] + self.slot(-1, half - 2)[...]
                return res
            way = 1 if k > 0 else -1
            length = half if way > 0 else half - 1
            s = length - abs(k)
            src = own
            if s > 0:
                self.last[way].wait_recv()
                src = self.slot(way, s - 1)
                src[...] = src[...] + own[...]
            self.last[way] = gcopy(src, self.slot(way, s), self.to[way * self.d])
            return None

    x_to, y_to = {1: x_up, -1: x_dn}, {1: y_up, -1: y_dn}

    def slots(ref, half):
        return lambda way, s: ref.at[s if way > 0 else half + s]

    base = 23.0

    def finish(kk, got, part):
        layer = zp + 4 * c + 2 * kk
        for cc in range(2):
            here = got.at[pl.ds(16 * cc, WIN)]
            there = fr[part].at[zh]
            i = 4 * part + 2 * kk + cc
            send = rc(here, there, ls.at[i], lr.at[4 * part + zh], dev(cc=cc, zz=layer))
            same = jnp.logical_and(layer == z, c == cc)
            last.append((send, same))

            @pl.when(jnp.logical_not(same))
            def _():
                send.start()

            @pl.when(same)
            def _():
                there[...] = here[...]

    last = []

    def chain_a(kk, j, second):
        d = 1 - 2 * kk
        k2 = Chains.deltas(NX)[j]
        q = mod(x + d * k2, NX)
        ring = Chains(NY, y, d, y_to, slots(ray.at[kk, j], NY // 2))
        t0 = base + 3.0 + 4.5 * j
        for i, k in enumerate(Chains.deltas(NY)):
            got = ring.step(k, ta.at[kk, rows_of(q, mod(y + d * k, NY))])
            if k < 0 or k == 1:
                yield t0 + 3.6 * (i // 2 + 1)
        got = second.step(k2, got)
        if k2 == 0:
            finish(kk, got, 0)

    def chain_b(kk, j, second):
        d = 1 - 2 * kk
        k2 = Chains.deltas(NY)[j]
        q = mod(y + d * k2, NY)
        ring = Chains(NX, x, d, x_to, slots(rbx.at[kk, j], NX // 2))
        t0 = base + 3.7 * j
        for i, k in enumerate(Chains.deltas(NX)):
            got = ring.step(k, tb.at[kk, rows_of(mod(x + d * k, NX), q)])
            if k == -1:
                yield t0 + 4.5
            elif k == 1:
                yield t0 + 8.5
        got = second.step(k2, got)
        if k2 == 0:
            finish(kk, got, 1)

    a_second = [Chains(NX, x, 1 - 2 * kk, x_to, slots(rax.at[kk], NX // 2)) for kk in range(2)]
    b_second = [Chains(NY, y, 1 - 2 * kk, y_to, slots(rby.at[kk], NY // 2)) for kk in range(2)]
    for j in range(8):
        for kk in range(2):
            put(chain_b(kk, j, b_second[kk]), base + 0.1 * kk + max(0, 3.7 * (j - 1)))
    for j in range(4):
        for kk in range(2):
            put(chain_a(kk, j, a_second[kk]), base + 3.0 + 0.1 * kk)
    ready(1, 19.0)
    terms(1, 0)
    run(base + 0.05)
    terms(1, 1)
    run(base + 0.15)
    ready(0, base + 0.2)
    terms(0, 0)
    run(base + 3.05)
    terms(0, 1)
    run(base + 3.15)

    store_fg = pltpu.make_async_copy(fgv, fg_ref, lsem.at[3])

    def outputs():
        now = base + 12
        while spreading[0]:
            now += 1
            yield now
        rest_there()
        back = []
        for kk in range(2):
            layer = zp + 4 * c + 2 * kk

            @pl.loop(0, 4)
            def _(i):
                fs[kk, place(i), :] = jnp.dot(kcot[kk, place(i), :], wbuf[pl.ds(2 * kk, 2)].reshape(C, HW),
                                              preferred_element_type=jnp.float32).astype(jnp.bfloat16)
            for p, to in ((2, dev(cc=0, zz=(z_dn, z_up)[kk])), (3, dev(cc=1, zz=(z_dn, z_up)[kk])), (1 - c, sib)):
                back.append(rc(fs.at[kk, place(p)], ret.at[layer], bs.at[len(back)], br.at[layer], to))
                back[-1].start()
            ret[layer] = fs[kk, place(c), :]
            if kk == 0:
                now += 3
                yield now
        pending.extend(back)
        yield now + 12
        for kk in range(2):
            for layer in (zp + 4 * (1 - c) + 2 * kk, away[kk][0], away[kk][1]):
                rc(fs.at[kk, place(0)], ret.at[layer], bs.at[0], br.at[layer], sib).wait_recv()
        for u in range(UD):
            fgv[u] = jnp.where(frame < counts[u], ret[host[z * UD + u]], jnp.zeros((FR, HW), jnp.bfloat16))
        store_fg.start()

    put(outputs(), base + 12)
    run(base + 1000)

    for part in range(2):
        for i in range(4):
            got = rc(fr[part].at[i], fr[part].at[i], ls.at[0], lr.at[4 * part + i], sib)

            @pl.when(jnp.logical_not(jnp.logical_and(zh == i, z // 4 == c)))
            def _():
                got.wait_recv()
    for part, cols in ((0, slice(0, CUT)), (1, slice(CUT, HW))):
        ref = fr[part]
        first = ref[0, 0:20, :] + ref[1, 0:20, :] + ref[2, 0:20, :] + ref[3, 0:20, :]
        second = ref[0, 4:24, :] + ref[1, 4:24, :] + ref[2, 4:24, :] + ref[3, 4:24, :]
        wg_ref[:, cols] = jnp.where(jnp.full(first.shape, c, jnp.int32) == 0, first, second).astype(jnp.bfloat16)

    for send, same in last:
        @pl.when(jnp.logical_not(same))
        def _():
            send.wait_send()

    for cp in pending:
        cp.wait_send()
    store_fg.wait()

    @pl.when(own_core)
    def _():
        for cp in wz:
            cp.wait_send()

    @pl.when(is_src)
    def _():
        for cp in wcp:
            cp.wait_send()


def local(saved_context, cotangent, out_proj, frame_counts, host_segment):
    bf, f32, dma = jnp.bfloat16, jnp.float32, pltpu.SemaphoreType.DMA
    smem, vmem, hbm = (pl.BlockSpec(memory_space=m) for m in (pltpu.SMEM, pltpu.VMEM, pl.ANY))
    fg, wg = pl.pallas_call(
        kernel,
        name="backward",
        out_shape=(jax.ShapeDtypeStruct((UD, FR, HW), bf), jax.ShapeDtypeStruct((20, HW), bf)),
        in_specs=[smem, smem, hbm, hbm, hbm],
        out_specs=(hbm, vmem),
        scratch_shapes=[
            pltpu.VMEM((UD, FR, HW), bf),
            pltpu.VMEM((UD, FR, C), bf),
            pltpu.VMEM((LAYERS, FR, CUT), bf),
            pltpu.VMEM((LAYERS, FR, HW - CUT), bf),
            pltpu.VMEM((LAYERS, FR, C), bf),
            pltpu.VMEM((2, KS, CUT), bf),
            pltpu.VMEM((2, KS, HW - CUT), bf),
            pltpu.VMEM((2, KS, C), bf),
            pltpu.VMEM((NX, NY, PIECE, HW), bf),
            pltpu.VMEM((2, C, CUT), f32),
            pltpu.VMEM((2, C, HW - CUT), f32),
            pltpu.VMEM((2, NX, NY - 1, ROWS, CUT), f32),
            pltpu.VMEM((2, NX - 1, ROWS, CUT), f32),
            pltpu.VMEM((2, NY, NX - 1, ROWS, HW - CUT), f32),
            pltpu.VMEM((2, NY - 1, ROWS, HW - CUT), f32),
            pltpu.VMEM((4, WIN, CUT), f32),
            pltpu.VMEM((4, WIN, HW - CUT), f32),
            pltpu.VMEM((2, KS, HW), bf),
            pltpu.VMEM((LAYERS, FR, HW), bf),
            pltpu.VMEM((UD, FR, HW), bf),
            dma((5,)),
            dma((24,)), dma((24,)),
            dma((80,)), dma((80,)),
            dma((128,)), dma((128,)),
            dma((10,)), dma((10,)),
            dma((8,)), dma((8,)),
        ],
        compiler_params=pltpu.CompilerParams(collective_id=0, has_side_effects=True, vmem_limit_bytes=56 << 20),
    )(host_segment, frame_counts, saved_context, cotangent, out_proj.reshape(2, NY, PIECE, HW))
    return fg, wg[None]


def solution(mesh):
    placed = (
        P(("dp", "segment"), None, None),
        P(("dp", "segment"), None, None),
        P("segment", None, None),
        P(("dp", "segment")),
        P("dp"),
    )
    return jax.shard_map(
        local,
        mesh=mesh,
        in_specs=placed,
        out_specs=(P(("dp", "segment"), None, None), P("segment", "dp", None)),
        check_vma=False,
    )
```

```python
import functools
import heapq

import jax
import jax.numpy as jnp
from jax import lax
from jax.experimental import pallas as pl
from jax.experimental.pallas import tpu as pltpu
from jax.sharding import PartitionSpec as P

MESH = pl.DeviceIdType.MESH
NX, NY, NC, NZ = 4, 8, 2, 8
C, HW, FR, UD = 1280, 640, 128, 4
LAYERS = 8
KS = 4 * FR
CUT = 256
PIECE = C * 2 // (NX * NY)
WA = 32
WB = 64
ROWS = C // (NX * NY)
WIN = 24


def kernel(host, counts, ctx, cot, w, fg_ref, wg_ref, uctx, ucot, pctxa, pctxb, pcot, kctxa, kctxb, kcot, wbuf, ta, tb, ray, rax, rbx,
           rby, fra, frb, fs, ret, fgv, lsem, us, ur, ws, wr, gs, gr, bs, br, ls, lr):
    kctx, pctx, t, fr = (kctxa, kctxb), (pctxa, pctxb), (ta, tb), (fra, frb)
    dp = lax.axis_index("dp")
    z = lax.axis_index("segment")
    x, y, c = dp // (NY * NC), lax.rem(dp // NC, NY), lax.rem(dp, NC)
    zp, zh = lax.rem(z, 2), z // 2

    def dev(xx=None, yy=None, cc=None, zz=None):
        xx, yy, cc, zz = (b if a is None else a for a, b in ((xx, x), (yy, y), (cc, c), (zz, z)))
        return ((xx * NY + yy) * NC + cc, zz)

    def mod(v, n):
        return lax.rem(v + 2 * n, n)

    z_up, z_dn = mod(z + 1, NZ), mod(z - 1, NZ)
    x_up, x_dn = dev(xx=mod(x + 1, NX)), dev(xx=mod(x - 1, NX))
    y_up, y_dn = dev(yy=mod(y + 1, NY)), dev(yy=mod(y - 1, NY))
    sib = dev(cc=1 - c)

    bar = pltpu.get_barrier_semaphore()
    x_far, y_up2, y_dn2 = dev(xx=mod(x + 2, NX)), dev(yy=mod(y + 2, NY)), dev(yy=mod(y - 2, NY))
    partners = [x_up, x_dn, y_up, y_dn, sib, x_far, y_up2, y_dn2]
    for d in (1, 2, 4, 6, 7):
        for cc in (c, 1 - c):
            partners.append(dev(cc=cc, zz=mod(z + d, NZ)))
    for p in partners:
        pl.semaphore_signal(bar, inc=1, device_id=p, device_id_type=MESH)

    load_ctx = pltpu.make_async_copy(ctx, uctx, lsem.at[0])
    load_cot = pltpu.make_async_copy(cot, ucot, lsem.at[1])
    load_ctx.start()
    load_cot.start()

    pl.semaphore_wait(bar, len(partners))

    def rc(src, dst, ssem, rsem, to):
        return pltpu.make_async_remote_copy(src_ref=src, dst_ref=dst, send_sem=ssem, recv_sem=rsem, device_id=to, device_id_type=MESH)

    kkp = x // 2
    wsrc = w.at[lax.rem(x, 2), y, pl.ds(0, WB)]
    wdst = wbuf.at[x, y, pl.ds(0, WB)]
    is_src = zh == 2 * c + kkp
    wcp = [rc(wsrc, wdst, ws.at[i], wr.at[0], dev(zz=mod(z + d, NZ))) for i, d in enumerate((2, 4, 6))]
    wlocal = pltpu.make_async_copy(wsrc, wdst, lsem.at[2])

    @pl.when(is_src)
    def _():
        for cp in wcp:
            cp.start()
        wlocal.start()

    kz, own_core = lax.rem(zh, 2), c == z // 4
    zrows = pl.ds(WB, PIECE - WB)
    wz_src, wz_dst = w.at[:, :, zrows], wbuf.at[pl.ds(2 * kz, 2), :, zrows]
    wz = [rc(wz_src, wz_dst, bs.at[6 + i], br.at[8 + kz], dev(zz=mod(z + d, NZ))) for i, d in enumerate((2, 6, 4))]
    wz_local = pltpu.make_async_copy(wz_src, wz_dst, lsem.at[4])

    def send_rest():
        @pl.when(own_core)
        def _():
            for cp in wz:
                cp.start()
            wz_local.start()
        yield 0

    def rest_there():
        @pl.when(own_core)
        def _():
            wz_local.wait()

        for kk in range(2):
            @pl.when(jnp.logical_not(jnp.logical_and(own_core, kz == kk)))
            def _():
                rc(wz_src, wbuf.at[pl.ds(2 * kk, 2), :, zrows], bs.at[6], br.at[8 + kk], sib).wait_recv()

    load_ctx.wait()
    load_cot.wait()
    frame = lax.broadcasted_iota(jnp.int32, (FR, HW), 0)

    def pack(layer):
        idx, valid = jnp.int32(0), jnp.int32(0)
        for u in range(UD):
            mine = host[z * UD + u] == layer
            idx = jnp.where(mine, jnp.int32(u), idx)
            valid = jnp.where(mine, jnp.int32(1), valid)
        pcot[layer] = ucot[idx]
        val = jnp.where(frame < counts[idx] * valid, uctx[idx], jnp.zeros((FR, HW), jnp.bfloat16))
        pctxa[layer] = val[:, 0:CUT]
        pctxb[layer] = val[:, CUT:HW]

    away = [[1 - zp + 4 * cc + 2 * kk for cc in range(2)] for kk in range(2)]
    for kk in range(2):
        for cc in range(2):
            pack(away[kk][cc])

    def place(p):
        return pl.ds(pl.multiple_of(p * FR, FR), FR)

    nu = [0]

    def ucopy(src, dst, rsem, to):
        i = nu[0]
        nu[0] += 1
        cp = rc(src, dst, us.at[i], ur.at[rsem], to)
        pending.append(cp)
        return cp

    pending = []
    half = FR // 2
    z_cot, z_ctx = [], ([], [])
    for kk in range(2):
        for cc in range(2):
            to = dev(cc=cc, zz=(z_up, z_dn)[kk])
            layer = away[kk][cc]
            for h in range(2):
                rows = pl.ds(pl.multiple_of((2 + c) * FR + h * half, half), half)
                z_cot.append(ucopy(pcot.at[layer, pl.ds(h * half, half)], kcot.at[kk, rows], 4 * kk + 2 * h + c, to))
            for part in range(2):
                z_ctx[part].append(ucopy(pctx[part].at[layer], kctx[part].at[kk, place(2 + c)], 8 + 4 * part + 2 * kk + c, to))
    for cp in z_cot:
        cp.start()
    near = []
    for kk in range(2):
        layer = zp + 4 * (1 - c) + 2 * kk
        pack(layer)
        near.append(ucopy(pcot.at[layer], kcot.at[kk, place(c)], 16 + kk, sib))
        for part in range(2):
            near.append(ucopy(pctx[part].at[layer], kctx[part].at[kk, place(c)], 18 + 2 * part + kk, sib))
    for cp in near:
        cp.start()
    for kk in range(2):
        layer = zp + 4 * c + 2 * kk
        pack(layer)
        kcot[kk, place(c), :] = pcot[layer]
        for part in range(2):
            kctx[part][kk, place(c), :] = pctx[part][layer]

    queue = []
    order = [0]

    def put(gen, when):
        heapq.heappush(queue, (when, order[0], gen))
        order[0] += 1

    def run(until):
        while queue and queue[0][0] < until:
            _, _, gen = heapq.heappop(queue)
            try:
                put(gen, next(gen))
            except StopIteration:
                pass

    wn = [3]

    spreading = [0]

    def track(gen):
        spreading[0] += 1
        yield from gen
        spreading[0] -= 1

    def wcopy(ref, to):
        i = wn[0]
        wn[0] += 1
        cp = rc(ref, ref, ws.at[i], wr.at[i], to)
        pending.append(cp)
        return cp

    HOP = 3.5

    def spread(n, me, up, dn, view, half, done, t0):
        far = n // 2
        ups, dns = [wcopy(view(me), up)], [wcopy(view(me), dn)]
        ups[0].start()
        dns[0].start()
        for s in range(1, far):
            for lst, to, sign in ((ups, up, 1), (dns, dn, -1)):
                t = t0 + HOP * s
                yield t
                ref = view(mod(me - sign * s, n))
                if s == far - 1:
                    ref = half(mod(me - sign * s, n), sign)
                cp = wcopy(ref, to)
                lst[-1].wait_recv()
                cp.start()
                lst.append(cp)
                done(-sign * s, t)
        t = t0 + HOP * far
        yield t
        ups[-1].wait_recv()
        dns[-1].wait_recv()
        done(far, t)

    def nothing(delta, t):
        pass

    def spread_x(view, done, t0):
        cps = [wcopy(view(x), to) for to in (x_up, x_dn, x_far)]
        for cp in cps:
            cp.start()
        for cp, delta in zip(cps, (-1, 1, 2)):
            yield t0 + HOP
            cp.wait_recv()
            done(delta, t0 + HOP)

    def spread_y(view, half, done, t0):
        cps = {k: wcopy(view(y), to) for k, to in ((1, y_up), (-1, y_dn), (2, y_up2), (-2, y_dn2))}
        for cp in cps.values():
            cp.start()
        for k in (1, -1):
            yield t0 + HOP
            cps[k].wait_recv()
            done(-k, t0 + HOP)
        more = {}
        for k in (1, -1):
            t = t0 + HOP + 0.5
            yield t
            b = mod(y - 2 * k, NY)
            more[k] = [wcopy(view(b), (y_up, y_dn)[k < 0]), wcopy(half(b, k), (y_up2, y_dn2)[k < 0])]
            cps[2 * k].wait_recv()
            for cp in more[k]:
                cp.start()
            done(-2 * k, t)
        for k in (1, -1):
            t = t0 + 2 * HOP + 0.5
            yield t
            more[k][0].wait_recv()
            done(-3 * k, t)
        t = t0 + 2 * HOP + 1
        yield t
        more[1][1].wait_recv()
        more[-1][1].wait_recv()
        done(4, t)

    a_rows, b_rows = pl.ds(0, WA), pl.ds(WA, WB - WA)

    def spread_ay(delta, t):
        b = mod(x + delta, NX)
        put(track(spread(NY, y, y_up, y_dn, lambda k: wbuf.at[b, k, a_rows],
                         lambda k, sign: wbuf.at[b, k, pl.ds(0 if sign > 0 else 16, 16)], nothing, t)), t)

    def spread_bx(delta, t):
        b = mod(y + delta, NY)

        put(track(spread(NX, x, x_up, x_dn, lambda k: wbuf.at[k, b, b_rows],
                         lambda k, sign: wbuf.at[k, b, pl.ds(WA if sign > 0 else WA + 16, 16)], nothing, t)), t)

    def weights():
        @pl.when(is_src)
        def _():
            wlocal.wait()

        @pl.when(jnp.logical_not(is_src))
        def _():
            wcp[0].wait_recv()

        put(track(spread_x(lambda b: wbuf.at[b, y, a_rows], spread_ay, W0)), W0)
        put(track(spread_y(lambda b: wbuf.at[x, b, b_rows],
                           lambda b, sign: wbuf.at[x, b, pl.ds(WA if sign > 0 else WA + 16, 16)], spread_bx, W0)), W0)
        spread_ay(0, W0)
        spread_bx(0, W0)
        yield W0

    def send_ctx():
        for cp in z_ctx[1] + z_ctx[0]:
            cp.start()
        yield 0

    W0 = 6.0
    put(weights(), W0)
    put(send_ctx(), 9.0)
    put(send_rest(), 17.0)

    def ready(part, t0):
        run(t0)
        for cp in near[1 + part::3]:
            cp.wait_recv()
        if part == 1:
            for cp in near[0::3]:
                cp.wait_recv()
        for kk in range(2):
            for src in range(2):
                if part == 1:
                    for h in range(2):
                        rows = pl.ds((2 + src) * FR + h * half, half)
                        rc(pcot.at[0, pl.ds(0, half)], kcot.at[kk, rows], us.at[0], ur.at[4 * kk + 2 * h + src], sib).wait_recv()
                there = kctx[part].at[kk, pl.ds((2 + src) * FR, FR)]
                rc(pctx[part].at[0], there, us.at[0], ur.at[8 + 4 * part + 2 * kk + src], sib).wait_recv()

    def terms(part, kk):
        @pl.loop(0, C // 256)
        def _(i):
            rows = pl.ds(pl.multiple_of(i * 256, 256), 256)
            t[part][kk, rows, :] = lax.dot_general(kcot[kk, :, rows], kctx[part][kk], (((0,), (0,)), ((), ())),
                                                   preferred_element_type=jnp.float32)

    gn = [0]

    def gcopy(src, dst, to):
        i = gn[0]
        gn[0] += 1
        cp = rc(src, dst, gs.at[i], gr.at[i], to)
        pending.append(cp)
        cp.start()
        return cp

    def rows_of(xb, yb):
        return pl.ds(pl.multiple_of((xb * NY + yb) * ROWS, 8), ROWS)

    class Chains:
        def __init__(self, n, me, d, to, slot):
            self.n, self.me, self.d, self.to, self.slot = n, me, d, to, slot
            self.last = {1: None, -1: None}

        @staticmethod
        def deltas(n):
            out = [n // 2]
            for k in range(n // 2 - 1, 0, -1):
                out += [-k, k]
            return out + [0]

        def step(self, k, own):
            half = self.n // 2
            if k == 0:
                for way in (1, -1):
                    self.last[way].wait_recv()
                res = self.slot(1, half - 1)
                res[...] = own[...] + res[...] + self.slot(-1, half - 2)[...]
                return res
            way = 1 if k > 0 else -1
            length = half if way > 0 else half - 1
            s = length - abs(k)
            src = own
            if s > 0:
                self.last[way].wait_recv()
                src = self.slot(way, s - 1)
                src[...] = src[...] + own[...]
            self.last[way] = gcopy(src, self.slot(way, s), self.to[way * self.d])
            return None

    x_to, y_to = {1: x_up, -1: x_dn}, {1: y_up, -1: y_dn}

    def slots(ref, half):
        return lambda way, s: ref.at[s if way > 0 else half + s]

    base = 23.0

    def finish(kk, got, part):
        layer = zp + 4 * c + 2 * kk
        for cc in range(2):
            here = got.at[pl.ds(16 * cc, WIN)]
            there = fr[part].at[zh]
            i = 4 * part + 2 * kk + cc
            send = rc(here, there, ls.at[i], lr.at[4 * part + zh], dev(cc=cc, zz=layer))
            same = jnp.logical_and(layer == z, c == cc)
            last.append((send, same))

            @pl.when(jnp.logical_not(same))
            def _():
                send.start()

            @pl.when(same)
            def _():
                there[...] = here[...]

    last = []

    def chain_a(kk, j, second):
        d = 1 - 2 * kk
        k2 = Chains.deltas(NX)[j]
        q = mod(x + d * k2, NX)
        ring = Chains(NY, y, d, y_to, slots(ray.at[kk, j], NY // 2))
        t0 = base + 3.0 + 5.5 * j
        for i, k in enumerate(Chains.deltas(NY)):
            got = ring.step(k, ta.at[kk, rows_of(q, mod(y + d * k, NY))])
            if k < 0 or k == 1:
                yield t0 + 3.6 * (i // 2 + 1)
        got = second.step(k2, got)
        if k2 == 0:
            finish(kk, got, 0)

    def chain_b(kk, j, second):
        d = 1 - 2 * kk
        k2 = Chains.deltas(NY)[j]
        q = mod(y + d * k2, NY)
        ring = Chains(NX, x, d, x_to, slots(rbx.at[kk, j], NX // 2))
        t0 = base + 3.7 * j
        for i, k in enumerate(Chains.deltas(NX)):
            got = ring.step(k, tb.at[kk, rows_of(mod(x + d * k, NX), q)])
            if k == -1:
                yield t0 + 4.5
            elif k == 1:
                yield t0 + 8.5
        got = second.step(k2, got)
        if k2 == 0:
            finish(kk, got, 1)

    a_second = [Chains(NX, x, 1 - 2 * kk, x_to, slots(rax.at[kk], NX // 2)) for kk in range(2)]
    b_second = [Chains(NY, y, 1 - 2 * kk, y_to, slots(rby.at[kk], NY // 2)) for kk in range(2)]
    for j in range(8):
        for kk in range(2):
            put(chain_b(kk, j, b_second[kk]), base + 0.1 * kk + max(0, 3.7 * (j - 1.3)))
    for j in range(4):
        for kk in range(2):
            put(chain_a(kk, j, a_second[kk]), base + 3.0 + 0.1 * kk)
    ready(1, 19.0)
    terms(1, 0)
    run(base + 0.05)
    terms(1, 1)
    run(base + 0.15)
    ready(0, base + 0.2)
    terms(0, 0)
    run(base + 3.05)
    terms(0, 1)
    run(base + 3.15)

    store_fg = pltpu.make_async_copy(fgv, fg_ref, lsem.at[3])

    def outputs():
        now = base + 15
        while spreading[0]:
            now += 1
            yield now
        rest_there()
        back = []
        for kk in range(2):
            layer = zp + 4 * c + 2 * kk

            @pl.loop(0, 4)
            def _(i):
                fs[kk, place(i), :] = jnp.dot(kcot[kk, place(i), :], wbuf[pl.ds(2 * kk, 2)].reshape(C, HW),
                                              preferred_element_type=jnp.float32).astype(jnp.bfloat16)
            for p, to in ((2, dev(cc=0, zz=(z_dn, z_up)[kk])), (3, dev(cc=1, zz=(z_dn, z_up)[kk])), (1 - c, sib)):
                back.append(rc(fs.at[kk, place(p)], ret.at[layer], bs.at[len(back)], br.at[layer], to))
                back[-1].start()
            ret[layer] = fs[kk, place(c), :]
            if kk == 0:
                now += 3
                yield now
        pending.extend(back)
        yield now + 12
        for kk in range(2):
            for layer in (zp + 4 * (1 - c) + 2 * kk, away[kk][0], away[kk][1]):
                rc(fs.at[kk, place(0)], ret.at[layer], bs.at[0], br.at[layer], sib).wait_recv()
        for u in range(UD):
            fgv[u] = jnp.where(frame < counts[u], ret[host[z * UD + u]], jnp.zeros((FR, HW), jnp.bfloat16))
        store_fg.start()

    put(outputs(), base + 15)
    run(base + 1000)

    for part in range(2):
        for i in range(4):
            got = rc(fr[part].at[i], fr[part].at[i], ls.at[0], lr.at[4 * part + i], sib)

            @pl.when(jnp.logical_not(jnp.logical_and(zh == i, z // 4 == c)))
            def _():
                got.wait_recv()
    for part, cols in ((0, slice(0, CUT)), (1, slice(CUT, HW))):
        ref = fr[part]
        first = ref[0, 0:20, :] + ref[1, 0:20, :] + ref[2, 0:20, :] + ref[3, 0:20, :]
        second = ref[0, 4:24, :] + ref[1, 4:24, :] + ref[2, 4:24, :] + ref[3, 4:24, :]
        wg_ref[:, cols] = jnp.where(jnp.full(first.shape, c, jnp.int32) == 0, first, second).astype(jnp.bfloat16)

    for send, same in last:
        @pl.when(jnp.logical_not(same))
        def _():
            send.wait_send()

    for cp in pending:
        cp.wait_send()
    store_fg.wait()

    @pl.when(own_core)
    def _():
        for cp in wz:
            cp.wait_send()

    @pl.when(is_src)
    def _():
        for cp in wcp:
            cp.wait_send()


def local(saved_context, cotangent, out_proj, frame_counts, host_segment):
    bf, f32, dma = jnp.bfloat16, jnp.float32, pltpu.SemaphoreType.DMA
    smem, vmem, hbm = (pl.BlockSpec(memory_space=m) for m in (pltpu.SMEM, pltpu.VMEM, pl.ANY))
    fg, wg = pl.pallas_call(
        kernel,
        name="backward",
        out_shape=(jax.ShapeDtypeStruct((UD, FR, HW), bf), jax.ShapeDtypeStruct((20, HW), bf)),
        in_specs=[smem, smem, hbm, hbm, hbm],
        out_specs=(hbm, vmem),
        scratch_shapes=[
            pltpu.VMEM((UD, FR, HW), bf),
            pltpu.VMEM((UD, FR, C), bf),
            pltpu.VMEM((LAYERS, FR, CUT), bf),
            pltpu.VMEM((LAYERS, FR, HW - CUT), bf),
            pltpu.VMEM((LAYERS, FR, C), bf),
            pltpu.VMEM((2, KS, CUT), bf),
            pltpu.VMEM((2, KS, HW - CUT), bf),
            pltpu.VMEM((2, KS, C), bf),
            pltpu.VMEM((NX, NY, PIECE, HW), bf),
            pltpu.VMEM((2, C, CUT), f32),
            pltpu.VMEM((2, C, HW - CUT), f32),
            pltpu.VMEM((2, NX, NY - 1, ROWS, CUT), f32),
            pltpu.VMEM((2, NX - 1, ROWS, CUT), f32),
            pltpu.VMEM((2, NY, NX - 1, ROWS, HW - CUT), f32),
            pltpu.VMEM((2, NY - 1, ROWS, HW - CUT), f32),
            pltpu.VMEM((4, WIN, CUT), f32),
            pltpu.VMEM((4, WIN, HW - CUT), f32),
            pltpu.VMEM((2, KS, HW), bf),
            pltpu.VMEM((LAYERS, FR, HW), bf),
            pltpu.VMEM((UD, FR, HW), bf),
            dma((5,)),
            dma((24,)), dma((24,)),
            dma((80,)), dma((80,)),
            dma((128,)), dma((128,)),
            dma((10,)), dma((10,)),
            dma((8,)), dma((8,)),
        ],
        compiler_params=pltpu.CompilerParams(collective_id=0, has_side_effects=True, vmem_limit_bytes=56 << 20),
    )(host_segment, frame_counts, saved_context, cotangent, out_proj.reshape(2, NY, PIECE, HW))
    return fg, wg[None]


def solution(mesh):
    placed = (
        P(("dp", "segment"), None, None),
        P(("dp", "segment"), None, None),
        P("segment", None, None),
        P(("dp", "segment")),
        P("dp"),
    )
    return jax.shard_map(
        local,
        mesh=mesh,
        in_specs=placed,
        out_specs=(P(("dp", "segment"), None, None), P("segment", "dp", None)),
        check_vma=False,
    )
```

```python
import functools
import heapq

import jax
import jax.numpy as jnp
from jax import lax
from jax.experimental import pallas as pl
from jax.experimental.pallas import tpu as pltpu
from jax.sharding import PartitionSpec as P

MESH = pl.DeviceIdType.MESH
NX, NY, NC, NZ = 4, 8, 2, 8
C, HW, FR, UD = 1280, 640, 128, 4
LAYERS = 8
KS = 4 * FR
CUT = 256
PIECE = C * 2 // (NX * NY)
WA = 32
WB = 64
ROWS = C // (NX * NY)
WIN = 24


def kernel(host, counts, ctx, cot, w, fg_ref, wg_ref, uctx, ucot, pctxa, pctxb, pcot, kctxa, kctxb, kcot, wbuf, ta, tb, ray, rax, rbx,
           rby, fra, frb, fs, ret, fgv, lsem, us, ur, ws, wr, gs, gr, bs, br, ls, lr):
    kctx, pctx, t, fr = (kctxa, kctxb), (pctxa, pctxb), (ta, tb), (fra, frb)
    dp = lax.axis_index("dp")
    z = lax.axis_index("segment")
    x, y, c = dp // (NY * NC), lax.rem(dp // NC, NY), lax.rem(dp, NC)
    zp, zh = lax.rem(z, 2), z // 2

    def dev(xx=None, yy=None, cc=None, zz=None):
        xx, yy, cc, zz = (b if a is None else a for a, b in ((xx, x), (yy, y), (cc, c), (zz, z)))
        return ((xx * NY + yy) * NC + cc, zz)

    def mod(v, n):
        return lax.rem(v + 2 * n, n)

    z_up, z_dn = mod(z + 1, NZ), mod(z - 1, NZ)
    x_up, x_dn = dev(xx=mod(x + 1, NX)), dev(xx=mod(x - 1, NX))
    y_up, y_dn = dev(yy=mod(y + 1, NY)), dev(yy=mod(y - 1, NY))
    sib = dev(cc=1 - c)

    bar = pltpu.get_barrier_semaphore()
    x_far, y_up2, y_dn2 = dev(xx=mod(x + 2, NX)), dev(yy=mod(y + 2, NY)), dev(yy=mod(y - 2, NY))
    partners = [x_up, x_dn, y_up, y_dn, sib, x_far, y_up2, y_dn2]
    for d in (1, 2, 4, 6, 7):
        for cc in (c, 1 - c):
            partners.append(dev(cc=cc, zz=mod(z + d, NZ)))
    for p in partners:
        pl.semaphore_signal(bar, inc=1, device_id=p, device_id_type=MESH)

    load_ctx = pltpu.make_async_copy(ctx, uctx, lsem.at[0])
    load_cot = pltpu.make_async_copy(cot, ucot, lsem.at[1])
    load_ctx.start()
    load_cot.start()

    pl.semaphore_wait(bar, len(partners))

    def rc(src, dst, ssem, rsem, to):
        return pltpu.make_async_remote_copy(src_ref=src, dst_ref=dst, send_sem=ssem, recv_sem=rsem, device_id=to, device_id_type=MESH)

    kkp = x // 2
    wsrc = w.at[lax.rem(x, 2), y, pl.ds(0, WB)]
    wdst = wbuf.at[x, y, pl.ds(0, WB)]
    is_src = zh == 2 * c + kkp
    wcp = [rc(wsrc, wdst, ws.at[i], wr.at[0], dev(zz=mod(z + d, NZ))) for i, d in enumerate((2, 4, 6))]
    wlocal = pltpu.make_async_copy(wsrc, wdst, lsem.at[2])

    @pl.when(is_src)
    def _():
        for cp in wcp:
            cp.start()
        wlocal.start()

    kz, own_core = lax.rem(zh, 2), c == z // 4
    zrows = pl.ds(WB, PIECE - WB)
    wz_src, wz_dst = w.at[:, :, zrows], wbuf.at[pl.ds(2 * kz, 2), :, zrows]
    wz = [rc(wz_src, wz_dst, bs.at[6 + i], br.at[8 + kz], dev(zz=mod(z + d, NZ))) for i, d in enumerate((2, 6, 4))]
    wz_local = pltpu.make_async_copy(wz_src, wz_dst, lsem.at[4])

    def send_rest():
        @pl.when(own_core)
        def _():
            for cp in wz:
                cp.start()
            wz_local.start()
        yield 0

    def rest_there():
        @pl.when(own_core)
        def _():
            wz_local.wait()

        for kk in range(2):
            @pl.when(jnp.logical_not(jnp.logical_and(own_core, kz == kk)))
            def _():
                rc(wz_src, wbuf.at[pl.ds(2 * kk, 2), :, zrows], bs.at[6], br.at[8 + kk], sib).wait_recv()

    load_ctx.wait()
    load_cot.wait()
    frame = lax.broadcasted_iota(jnp.int32, (FR, HW), 0)

    def pack(layer):
        idx, valid = jnp.int32(0), jnp.int32(0)
        for u in range(UD):
            mine = host[z * UD + u] == layer
            idx = jnp.where(mine, jnp.int32(u), idx)
            valid = jnp.where(mine, jnp.int32(1), valid)
        pcot[layer] = ucot[idx]
        val = jnp.where(frame < counts[idx] * valid, uctx[idx], jnp.zeros((FR, HW), jnp.bfloat16))
        pctxa[layer] = val[:, 0:CUT]
        pctxb[layer] = val[:, CUT:HW]

    away = [[1 - zp + 4 * cc + 2 * kk for cc in range(2)] for kk in range(2)]
    for kk in range(2):
        for cc in range(2):
            pack(away[kk][cc])

    def place(p):
        return pl.ds(pl.multiple_of(p * FR, FR), FR)

    nu = [0]

    def ucopy(src, dst, rsem, to):
        i = nu[0]
        nu[0] += 1
        cp = rc(src, dst, us.at[i], ur.at[rsem], to)
        pending.append(cp)
        return cp

    pending = []
    half = FR // 2
    z_cot, z_ctx = [], ([], [])
    for kk in range(2):
        for cc in range(2):
            to = dev(cc=cc, zz=(z_up, z_dn)[kk])
            layer = away[kk][cc]
            for h in range(2):
                rows = pl.ds(pl.multiple_of((2 + c) * FR + h * half, half), half)
                z_cot.append(ucopy(pcot.at[layer, pl.ds(h * half, half)], kcot.at[kk, rows], 4 * kk + 2 * h + c, to))
            for part in range(2):
                z_ctx[part].append(ucopy(pctx[part].at[layer], kctx[part].at[kk, place(2 + c)], 8 + 4 * part + 2 * kk + c, to))
    for cp in z_cot:
        cp.start()
    near = []
    for kk in range(2):
        layer = zp + 4 * (1 - c) + 2 * kk
        pack(layer)
        near.append(ucopy(pcot.at[layer], kcot.at[kk, place(c)], 16 + kk, sib))
        for part in range(2):
            near.append(ucopy(pctx[part].at[layer], kctx[part].at[kk, place(c)], 18 + 2 * part + kk, sib))
    for cp in near:
        cp.start()
    for kk in range(2):
        layer = zp + 4 * c + 2 * kk
        pack(layer)
        kcot[kk, place(c), :] = pcot[layer]
        for part in range(2):
            kctx[part][kk, place(c), :] = pctx[part][layer]

    queue = []
    order = [0]

    def put(gen, when):
        heapq.heappush(queue, (when, order[0], gen))
        order[0] += 1

    def run(until):
        while queue and queue[0][0] < until:
            _, _, gen = heapq.heappop(queue)
            try:
                put(gen, next(gen))
            except StopIteration:
                pass

    wn = [3]

    spreading = [0]

    def track(gen):
        spreading[0] += 1
        yield from gen
        spreading[0] -= 1

    def wcopy(ref, to):
        i = wn[0]
        wn[0] += 1
        cp = rc(ref, ref, ws.at[i], wr.at[i], to)
        pending.append(cp)
        return cp

    HOP = 3.5

    def spread(n, me, up, dn, view, half, done, t0):
        far = n // 2
        ups, dns = [wcopy(view(me), up)], [wcopy(view(me), dn)]
        ups[0].start()
        dns[0].start()
        for s in range(1, far):
            for lst, to, sign in ((ups, up, 1), (dns, dn, -1)):
                t = t0 + HOP * s
                yield t
                ref = view(mod(me - sign * s, n))
                if s == far - 1:
                    ref = half(mod(me - sign * s, n), sign)
                cp = wcopy(ref, to)
                lst[-1].wait_recv()
                cp.start()
                lst.append(cp)
                done(-sign * s, t)
        t = t0 + HOP * far
        yield t
        ups[-1].wait_recv()
        dns[-1].wait_recv()
        done(far, t)

    def nothing(delta, t):
        pass

    def spread_x(view, done, t0):
        cps = [wcopy(view(x), to) for to in (x_up, x_dn, x_far)]
        for cp in cps:
            cp.start()
        for cp, delta in zip(cps, (-1, 1, 2)):
            yield t0 + HOP
            cp.wait_recv()
            done(delta, t0 + HOP)

    def spread_y(view, half, done, t0):
        cps = {k: wcopy(view(y), to) for k, to in ((1, y_up), (-1, y_dn), (2, y_up2), (-2, y_dn2))}
        for cp in cps.values():
            cp.start()
        for k in (1, -1):
            yield t0 + HOP
            cps[k].wait_recv()
            done(-k, t0 + HOP)
        more = {}
        for k in (1, -1):
            t = t0 + HOP + 0.5
            yield t
            b = mod(y - 2 * k, NY)
            more[k] = [wcopy(view(b), (y_up, y_dn)[k < 0]), wcopy(half(b, k), (y_up2, y_dn2)[k < 0])]
            cps[2 * k].wait_recv()
            for cp in more[k]:
                cp.start()
            done(-2 * k, t)
        for k in (1, -1):
            t = t0 + 2 * HOP + 0.5
            yield t
            more[k][0].wait_recv()
            done(-3 * k, t)
        t = t0 + 2 * HOP + 1
        yield t
        more[1][1].wait_recv()
        more[-1][1].wait_recv()
        done(4, t)

    a_rows, b_rows = pl.ds(0, WA), pl.ds(WA, WB - WA)

    def spread_ay(delta, t):
        b = mod(x + delta, NX)
        put(track(spread(NY, y, y_up, y_dn, lambda k: wbuf.at[b, k, a_rows],
                         lambda k, sign: wbuf.at[b, k, pl.ds(0 if sign > 0 else 16, 16)], nothing, t)), t)

    def spread_bx(delta, t):
        b = mod(y + delta, NY)

        put(track(spread(NX, x, x_up, x_dn, lambda k: wbuf.at[k, b, b_rows],
                         lambda k, sign: wbuf.at[k, b, pl.ds(WA if sign > 0 else WA + 16, 16)], nothing, t)), t)

    def weights():
        @pl.when(is_src)
        def _():
            wlocal.wait()

        @pl.when(jnp.logical_not(is_src))
        def _():
            wcp[0].wait_recv()

        put(track(spread_x(lambda b: wbuf.at[b, y, a_rows], spread_ay, W0)), W0)
        put(track(spread_y(lambda b: wbuf.at[x, b, b_rows],
                           lambda b, sign: wbuf.at[x, b, pl.ds(WA if sign > 0 else WA + 16, 16)], spread_bx, W0)), W0)
        spread_ay(0, W0)
        spread_bx(0, W0)
        yield W0

    def send_ctx():
        for cp in z_ctx[1] + z_ctx[0]:
            cp.start()
        yield 0

    W0 = 6.0
    put(weights(), W0)
    put(send_ctx(), 9.0)
    put(send_rest(), 17.0)

    def ready(part, t0):
        run(t0)
        for cp in near[1 + part::3]:
            cp.wait_recv()
        if part == 1:
            for cp in near[0::3]:
                cp.wait_recv()
        for kk in range(2):
            for src in range(2):
                if part == 1:
                    for h in range(2):
                        rows = pl.ds((2 + src) * FR + h * half, half)
                        rc(pcot.at[0, pl.ds(0, half)], kcot.at[kk, rows], us.at[0], ur.at[4 * kk + 2 * h + src], sib).wait_recv()
                there = kctx[part].at[kk, pl.ds((2 + src) * FR, FR)]
                rc(pctx[part].at[0], there, us.at[0], ur.at[8 + 4 * part + 2 * kk + src], sib).wait_recv()

    def terms(part, kk):
        @pl.loop(0, 2)
        def _(i):
            rows = pl.ds(pl.multiple_of(i * (C // 2), 128), C // 2)
            t[part][kk, rows, :] = lax.dot_general(kcot[kk, :, rows], kctx[part][kk], (((0,), (0,)), ((), ())),
                                                   preferred_element_type=jnp.float32)

    gn = [0]

    def gcopy(src, dst, to):
        i = gn[0]
        gn[0] += 1
        cp = rc(src, dst, gs.at[i], gr.at[i], to)
        pending.append(cp)
        cp.start()
        return cp

    def rows_of(xb, yb):
        return pl.ds(pl.multiple_of((xb * NY + yb) * ROWS, 8), ROWS)

    class Chains:
        def __init__(self, n, me, d, to, slot):
            self.n, self.me, self.d, self.to, self.slot = n, me, d, to, slot
            self.last = {1: None, -1: None}

        @staticmethod
        def deltas(n):
            out = [n // 2]
            for k in range(n // 2 - 1, 0, -1):
                out += [-k, k]
            return out + [0]

        def step(self, k, own):
            half = self.n // 2
            if k == 0:
                for way in (1, -1):
                    self.last[way].wait_recv()
                res = self.slot(1, half - 1)
                res[...] = own[...] + res[...] + self.slot(-1, half - 2)[...]
                return res
            way = 1 if k > 0 else -1
            length = half if way > 0 else half - 1
            s = length - abs(k)
            src = own
            if s > 0:
                self.last[way].wait_recv()
                src = self.slot(way, s - 1)
                src[...] = src[...] + own[...]
            self.last[way] = gcopy(src, self.slot(way, s), self.to[way * self.d])
            return None

    x_to, y_to = {1: x_up, -1: x_dn}, {1: y_up, -1: y_dn}

    def slots(ref, half):
        return lambda way, s: ref.at[s if way > 0 else half + s]

    base = 23.0

    def finish(kk, got, part):
        layer = zp + 4 * c + 2 * kk
        for cc in range(2):
            here = got.at[pl.ds(16 * cc, WIN)]
            there = fr[part].at[zh]
            i = 4 * part + 2 * kk + cc
            send = rc(here, there, ls.at[i], lr.at[4 * part + zh], dev(cc=cc, zz=layer))
            same = jnp.logical_and(layer == z, c == cc)
            last.append((send, same))

            @pl.when(jnp.logical_not(same))
            def _():
                send.start()

            @pl.when(same)
            def _():
                there[...] = here[...]

    last = []

    def chain_a(kk, j, second):
        d = 1 - 2 * kk
        k2 = Chains.deltas(NX)[j]
        q = mod(x + d * k2, NX)
        ring = Chains(NY, y, d, y_to, slots(ray.at[kk, j], NY // 2))
        t0 = base + 3.0 + 5.5 * j
        for i, k in enumerate(Chains.deltas(NY)):
            got = ring.step(k, ta.at[kk, rows_of(q, mod(y + d * k, NY))])
            if k < 0 or k == 1:
                yield t0 + 3.6 * (i // 2 + 1)
        got = second.step(k2, got)
        if k2 == 0:
            finish(kk, got, 0)

    def chain_b(kk, j, second):
        d = 1 - 2 * kk
        k2 = Chains.deltas(NY)[j]
        q = mod(y + d * k2, NY)
        ring = Chains(NX, x, d, x_to, slots(rbx.at[kk, j], NX // 2))
        t0 = base + 3.7 * j
        for i, k in enumerate(Chains.deltas(NX)):
            got = ring.step(k, tb.at[kk, rows_of(mod(x + d * k, NX), q)])
            if k == -1:
                yield t0 + 4.5
            elif k == 1:
                yield t0 + 8.5
        got = second.step(k2, got)
        if k2 == 0:
            finish(kk, got, 1)

    a_second = [Chains(NX, x, 1 - 2 * kk, x_to, slots(rax.at[kk], NX // 2)) for kk in range(2)]
    b_second = [Chains(NY, y, 1 - 2 * kk, y_to, slots(rby.at[kk], NY // 2)) for kk in range(2)]
    for j in range(8):
        for kk in range(2):
            put(chain_b(kk, j, b_second[kk]), base + 0.1 * kk + max(0, 3.7 * (j - 1.3)))
    for j in range(4):
        for kk in range(2):
            put(chain_a(kk, j, a_second[kk]), base + 3.0 + 0.1 * kk)
    ready(1, 19.0)
    terms(1, 0)
    run(base + 0.05)
    terms(1, 1)
    run(base + 0.15)
    ready(0, base + 0.2)
    terms(0, 0)
    run(base + 3.05)
    terms(0, 1)
    run(base + 3.15)

    store_fg = pltpu.make_async_copy(fgv, fg_ref, lsem.at[3])

    def outputs():
        now = base + 15
        while spreading[0]:
            now += 1
            yield now
        rest_there()
        back = []
        for kk in range(2):
            layer = zp + 4 * c + 2 * kk

            @pl.loop(0, 2)
            def _(i):
                two = pl.ds(pl.multiple_of(i * 2 * FR, 2 * FR), 2 * FR)
                fs[kk, two, :] = jnp.dot(kcot[kk, two, :], wbuf[pl.ds(2 * kk, 2)].reshape(C, HW),
                                              preferred_element_type=jnp.float32).astype(jnp.bfloat16)
            for p, to in ((2, dev(cc=0, zz=(z_dn, z_up)[kk])), (3, dev(cc=1, zz=(z_dn, z_up)[kk])), (1 - c, sib)):
                back.append(rc(fs.at[kk, place(p)], ret.at[layer], bs.at[len(back)], br.at[layer], to))
                back[-1].start()
            ret[layer] = fs[kk, place(c), :]
            if kk == 0:
                now += 3
                yield now
        pending.extend(back)
        yield now + 12
        for kk in range(2):
            for layer in (zp + 4 * (1 - c) + 2 * kk, away[kk][0], away[kk][1]):
                rc(fs.at[kk, place(0)], ret.at[layer], bs.at[0], br.at[layer], sib).wait_recv()
        for u in range(UD):
            fgv[u] = jnp.where(frame < counts[u], ret[host[z * UD + u]], jnp.zeros((FR, HW), jnp.bfloat16))
        store_fg.start()

    put(outputs(), base + 15)
    run(base + 1000)

    for part in range(2):
        for i in range(4):
            got = rc(fr[part].at[i], fr[part].at[i], ls.at[0], lr.at[4 * part + i], sib)

            @pl.when(jnp.logical_not(jnp.logical_and(zh == i, z // 4 == c)))
            def _():
                got.wait_recv()
    for part, cols in ((0, slice(0, CUT)), (1, slice(CUT, HW))):
        ref = fr[part]
        first = ref[0, 0:20, :] + ref[1, 0:20, :] + ref[2, 0:20, :] + ref[3, 0:20, :]
        second = ref[0, 4:24, :] + ref[1, 4:24, :] + ref[2, 4:24, :] + ref[3, 4:24, :]
        wg_ref[:, cols] = jnp.where(jnp.full(first.shape, c, jnp.int32) == 0, first, second).astype(jnp.bfloat16)

    for send, same in last:
        @pl.when(jnp.logical_not(same))
        def _():
            send.wait_send()

    for cp in pending:
        cp.wait_send()
    store_fg.wait()

    @pl.when(own_core)
    def _():
        for cp in wz:
            cp.wait_send()

    @pl.when(is_src)
    def _():
        for cp in wcp:
            cp.wait_send()


def local(saved_context, cotangent, out_proj, frame_counts, host_segment):
    bf, f32, dma = jnp.bfloat16, jnp.float32, pltpu.SemaphoreType.DMA
    smem, vmem, hbm = (pl.BlockSpec(memory_space=m) for m in (pltpu.SMEM, pltpu.VMEM, pl.ANY))
    fg, wg = pl.pallas_call(
        kernel,
        name="backward",
        out_shape=(jax.ShapeDtypeStruct((UD, FR, HW), bf), jax.ShapeDtypeStruct((20, HW), bf)),
        in_specs=[smem, smem, hbm, hbm, hbm],
        out_specs=(hbm, vmem),
        scratch_shapes=[
            pltpu.VMEM((UD, FR, HW), bf),
            pltpu.VMEM((UD, FR, C), bf),
            pltpu.VMEM((LAYERS, FR, CUT), bf),
            pltpu.VMEM((LAYERS, FR, HW - CUT), bf),
            pltpu.VMEM((LAYERS, FR, C), bf),
            pltpu.VMEM((2, KS, CUT), bf),
            pltpu.VMEM((2, KS, HW - CUT), bf),
            pltpu.VMEM((2, KS, C), bf),
            pltpu.VMEM((NX, NY, PIECE, HW), bf),
            pltpu.VMEM((2, C, CUT), f32),
            pltpu.VMEM((2, C, HW - CUT), f32),
            pltpu.VMEM((2, NX, NY - 1, ROWS, CUT), f32),
            pltpu.VMEM((2, NX - 1, ROWS, CUT), f32),
            pltpu.VMEM((2, NY, NX - 1, ROWS, HW - CUT), f32),
            pltpu.VMEM((2, NY - 1, ROWS, HW - CUT), f32),
            pltpu.VMEM((4, WIN, CUT), f32),
            pltpu.VMEM((4, WIN, HW - CUT), f32),
            pltpu.VMEM((2, KS, HW), bf),
            pltpu.VMEM((LAYERS, FR, HW), bf),
            pltpu.VMEM((UD, FR, HW), bf),
            dma((5,)),
            dma((24,)), dma((24,)),
            dma((80,)), dma((80,)),
            dma((128,)), dma((128,)),
            dma((10,)), dma((10,)),
            dma((8,)), dma((8,)),
        ],
        compiler_params=pltpu.CompilerParams(collective_id=0, has_side_effects=True, vmem_limit_bytes=56 << 20),
    )(host_segment, frame_counts, saved_context, cotangent, out_proj.reshape(2, NY, PIECE, HW))
    return fg, wg[None]


def solution(mesh):
    placed = (
        P(("dp", "segment"), None, None),
        P(("dp", "segment"), None, None),
        P("segment", None, None),
        P(("dp", "segment")),
        P("dp"),
    )
    return jax.shard_map(
        local,
        mesh=mesh,
        in_specs=placed,
        out_specs=(P(("dp", "segment"), None, None), P("segment", "dp", None)),
        check_vma=False,
    )
```
